256 devices in a mesh: dp: 16 (over x_hi, z), tensor: 16 (over y, x_lo, core).
Axes of the slice: x: 4 (x_hi: 2, x_lo: 2; x = x_hi * 2 + x_lo), y: 4, z: 8, core: 2. Of those that a mesh axis runs over, the one named last changes fastest.
Arguments:
- hidden: bfloat16 [32768, 14336], P(('dp', 'tensor')), parts along dimension 0, may hold values from -6 to 6
- down_weight: bfloat16 [14336, 4096], P('tensor'), may hold values from -0.046875 to 0.046875
- residual: bfloat16 [32768, 4096], P(('dp', 'tensor')), parts along dimension 0, may hold values from -6 to 6
- row_order: int32 [32768], P('dp'), parts along dimension 0, may hold values from 0 to 2047, each once
- value_head: bfloat16 [4096], replicated, may hold values from -0.09375 to 0.09375
Outputs:
- layer_out: bfloat16 [32768, 4096], P(('dp', 'tensor')), parts along dimension 0
- scores: float32 [32768], P(('dp', 'tensor')), parts along dimension 0
The draws below stay inside these ranges and needn't reach their ends.
There are 16 independent parts, one for each index of `dp`. The reference program is written for one: setup_inputs(seed, part) draws one part's arguments, and reference() takes and returns one part's arrays. A program takes and returns all parts, laid end to end along the dimension named above; an argument that names none is the same for every part. Nothing has to cross between parts.
Inputs may be any that keep to these rules, and one draw needn't show every extreme that they name: `row_order`: each of the 2048 rollout rows appears exactly once.
All inputs are finite; a program needn't handle non-finite values.
Results may differ from the reference program's by a relative error of at most 0.02.
Values may be sent and summed in bfloat16 or wider, within the bound.
No kernel may reach another device: no remote copies, remote signals or barrier semaphores. Data moves between devices by JAX's collectives and lax.ppermute only.
A program may use at most 128 MiB of HBM per device.

```python
import jax
import jax.numpy as jnp
from jax import lax

D = 4096
FF = 14336
TOKENS = 2048
N_TENSOR = 16


def steps_of(own_key, extent, shards, least, largest):
    loudness, own = 1.0, jax.random.fold_in(own_key, 6)
    for axis_at, shards_of in shards:
        heights = jnp.exp(jax.random.uniform(jax.random.fold_in(own, axis_at), (shards_of,), jnp.float32, least / len(shards), largest / len(shards)))
        loudness = loudness * jnp.repeat(heights, extent[axis_at] // shards_of).reshape([-1 if axis == axis_at else 1 for axis in range(len(extent))])
    return loudness


def noise(stream_key, extent, spread, limit, split=(), dtype=jnp.bfloat16):
    factor_of = steps_of(stream_key, extent, split, -0.22, 0.18) if split else 1.0
    entries = jax.random.normal(stream_key, extent, jnp.float32) * spread * factor_of
    return jnp.minimum(jnp.maximum(entries, -limit), limit).astype(dtype)


def setup_inputs(seed: int = 0, part: int = 0) -> dict:
    splits = jax.random.split(jax.random.key(seed), 6)
    part_splits = jax.random.split(jax.random.fold_in(splits[5], part), 6)
    return {
        "hidden": noise(part_splits[0], (TOKENS, FF), 1.0, 6.0, ((0, 16),)),
        "down_weight": noise(splits[1], (FF, D), FF ** -0.5, 0.046875, ((0, 16),)),
        "residual": noise(part_splits[2], (TOKENS, D), 1.0, 6.0, ((0, 16),)),
        "row_order": jax.random.permutation(part_splits[3], TOKENS).astype(jnp.int32),
        "value_head": noise(splits[4], (D,), D ** -0.5, 0.09375),
    }


def reference(hidden, down_weight, residual, row_order, value_head):
    packed = jnp.take(hidden, row_order.astype(jnp.int32), axis=0)
    shard_width = FF // N_TENSOR
    hidden_blocks = packed.reshape(TOKENS, N_TENSOR, shard_width).transpose(1, 0, 2)
    weight_blocks = down_weight.reshape(N_TENSOR, shard_width, D)

    def accumulate(running, block_pair):
        block_term = jnp.dot(block_pair[0], block_pair[1], preferred_element_type=jnp.float32)
        rounded = lax.optimization_barrier(block_term.astype(jnp.bfloat16))
        return (running + rounded.astype(jnp.float32), None)
    down, _ = lax.scan(accumulate, jnp.zeros((TOKENS, D), jnp.float32), (hidden_blocks, weight_blocks))
    layer_out = (residual.astype(jnp.float32) + down).astype(jnp.bfloat16)
    widened = layer_out.astype(jnp.float32)
    mean_square = lax.optimization_barrier(jnp.mean(widened * widened, axis=-1, keepdims=True))
    normed = widened * lax.rsqrt(mean_square + 1e-05)
    scores = lax.optimization_barrier(jnp.sum(normed * value_head.astype(jnp.float32)[None, :], axis=-1))
    return (layer_out, scores)
```

```python
import functools

import jax
import jax.numpy as jnp
from jax import lax
from jax.experimental import pallas as pl
from jax.experimental.pallas import tpu as pltpu
from jax.sharding import PartitionSpec as P

NY, NX, NC = 4, 2, 2
TILE = 256
A_TILES, B1_TILES, B2_TILES = 7, 5, 4
WA, WB1, WB2 = A_TILES * TILE, B1_TILES * TILE, B2_TILES * TILE
WA1 = 3 * TILE
MIB = 1 << 20


def hop(value, dy, dx, dc):
    pairs = []
    for y in range(NY):
        for x in range(NX):
            for c in range(NC):
                source = (y * NX + x) * NC + c
                target = ((y + dy) % NY * NX + (x + dx) % NX) * NC + (c + dc) % NC
                pairs.append((source, target))
    return lax.ppermute(value, "tensor", pairs)


def gather_kernel(order_ref, rows_ref, out_ref):
    order = order_ref[...]
    at = lax.broadcasted_iota(jnp.int32, (order.shape[0], rows_ref.shape[0]), 1)
    pick = jnp.where(at == order, 1.0, 0.0).astype(jnp.bfloat16)
    out_ref[...] = jnp.dot(
        pick, rows_ref[...], preferred_element_type=jnp.float32
    ).astype(jnp.bfloat16)


def gather(order, rows):
    n, (m, k) = order.shape[0], rows.shape
    return pl.pallas_call(
        gather_kernel,
        grid=(n // 256,),
        in_specs=[
            pl.BlockSpec((256, 1), lambda i: (i, 0)),
            pl.BlockSpec((m, k), lambda i: (0, 0)),
        ],
        out_specs=pl.BlockSpec((256, k), lambda i: (i, 0)),
        out_shape=jax.ShapeDtypeStruct((n, k), jnp.bfloat16),
        compiler_params=pltpu.CompilerParams(vmem_limit_bytes=32 * MIB),
        cost_estimate=pl.CostEstimate(
            flops=2 * n * m * k, bytes_accessed=2 * (m * k + n * k), transcendentals=0
        ),
    )(order, rows)


def term_kernel(split_b, own_ref, sib_ref, w_own_ref, w_sib_ref, *outs):
    j = pl.program_id(0)
    total = jnp.dot(own_ref[...], w_own_ref[...], preferred_element_type=jnp.float32)
    total += jnp.dot(sib_ref[...], w_sib_ref[...], preferred_element_type=jnp.float32)
    total = total.astype(jnp.bfloat16)

    @pl.when(j < A_TILES)
    def _():
        outs[0][...] = total[:128]
        outs[1][...] = total[128:]

    if split_b:

        @pl.when(jnp.logical_and(j >= A_TILES, j < A_TILES + B1_TILES))
        def _():
            outs[2][...] = total[:128]
            outs[3][...] = total[128:]

        @pl.when(j >= A_TILES + B1_TILES)
        def _():
            outs[4][...] = total[:128]
            outs[5][...] = total[128:]

    else:

        @pl.when(j >= A_TILES)
        def _():
            outs[2][...] = total[:128]
            outs[3][...] = total[128:]


def term(own, sib, w_own, w_sib, split_b):
    k, d = w_own.shape
    tiles = d // TILE
    if split_b:
        ranges = [(0, A_TILES), (A_TILES, B1_TILES), (A_TILES + B1_TILES, B2_TILES)]
    else:
        ranges = [(0, A_TILES), (A_TILES, B1_TILES + B2_TILES)]

    def out_spec(first, count):
        return pl.BlockSpec((128, TILE), lambda j: (0, jnp.clip(j - first, 0, count - 1)))

    return pl.pallas_call(
        functools.partial(term_kernel, split_b),
        grid=(tiles,),
        in_specs=[
            pl.BlockSpec((256, k), lambda j: (0, 0)),
            pl.BlockSpec((256, k), lambda j: (0, 0)),
            pl.BlockSpec((k, TILE), lambda j: (0, j)),
            pl.BlockSpec((k, TILE), lambda j: (0, j)),
        ],
        out_specs=[out_spec(*r) for r in ranges for _ in range(2)],
        out_shape=[
            jax.ShapeDtypeStruct((128, r[1] * TILE), jnp.bfloat16) for r in ranges for _ in range(2)
        ],
        compiler_params=pltpu.CompilerParams(vmem_limit_bytes=32 * MIB),
        cost_estimate=pl.CostEstimate(
            flops=2 * 256 * 2 * k * d,
            bytes_accessed=2 * (2 * k * d + 256 * d + 512 * k),
            transcendentals=0,
        ),
    )(own, sib, w_own, w_sib)


def whole_call(kernel, out_shape, *args):
    n_bytes = sum(a.size * a.dtype.itemsize for a in args)
    return pl.pallas_call(
        kernel,
        out_shape=out_shape,
        compiler_params=pltpu.CompilerParams(vmem_limit_bytes=32 * MIB),
        cost_estimate=pl.CostEstimate(flops=n_bytes, bytes_accessed=2 * n_bytes, transcendentals=0),
    )(*args)


def f32(ref):
    return ref[...].astype(jnp.float32)


def bf(shape):
    return jax.ShapeDtypeStruct(shape, jnp.bfloat16)


def add_left_kernel(w, base_ref, come_ref, out_ref):
    out_ref[:, :w] = (base_ref[:, :w].astype(jnp.float32) + f32(come_ref)).astype(jnp.bfloat16)
    out_ref[:, w:] = base_ref[:, w:]


def add_right_kernel(w, base_ref, come_ref, out_ref):
    out_ref[:, :w] = base_ref[:, :w]
    out_ref[:, w:] = (base_ref[:, w:].astype(jnp.float32) + f32(come_ref)).astype(jnp.bfloat16)


def add_part(base, come, left):
    if left:
        kernel = functools.partial(add_left_kernel, come.shape[1])
    else:
        kernel = functools.partial(add_right_kernel, base.shape[1] - come.shape[1])
    return whole_call(kernel, bf(base.shape), base, come)


def split_sum_kernel(w, base_ref, come_ref, left_ref, right_ref):
    left_ref[...] = (
        base_ref[:, :w].astype(jnp.float32) + come_ref[:, :w].astype(jnp.float32)
    ).astype(jnp.bfloat16)
    right_ref[...] = (
        base_ref[:, w:].astype(jnp.float32) + come_ref[:, w:].astype(jnp.float32)
    ).astype(jnp.bfloat16)


def split_sum(base, come, w):
    n, m = base.shape
    return whole_call(
        functools.partial(split_sum_kernel, w), [bf((n, w)), bf((n, m - w))], base, come
    )


def sum3_part_kernel(w, left, base_ref, x_ref, come_ref, out_ref):
    total = f32(base_ref) + f32(x_ref)
    if left:
        out_ref[:, :w] = (total[:, :w] + f32(come_ref)).astype(jnp.bfloat16)
        out_ref[:, w:] = total[:, w:].astype(jnp.bfloat16)
    else:
        out_ref[:, :w] = total[:, :w].astype(jnp.bfloat16)
        out_ref[:, w:] = (total[:, w:] + f32(come_ref)).astype(jnp.bfloat16)


def sum3_part(base, x_come, come, left):
    w = come.shape[1] if left else base.shape[1] - come.shape[1]
    return whole_call(
        functools.partial(sum3_part_kernel, w, left), bf(base.shape), base, x_come, come
    )


def sum3_kernel(a_ref, b_ref, c_ref, out_ref):
    out_ref[...] = (f32(a_ref) + f32(b_ref) + f32(c_ref)).astype(jnp.bfloat16)


def last_kernel(
    wa, a0, a1, a2, a3, b0, b1, b2, b3, residual_ref, head_ref, out_ref, score_ref
):
    down_a = f32(a0) + f32(a1) + f32(a2) + f32(a3)
    down_b = f32(b0) + f32(b1) + f32(b2) + f32(b3)
    out_a = (residual_ref[:, :wa].astype(jnp.float32) + down_a).astype(jnp.bfloat16)
    out_b = (residual_ref[:, wa:].astype(jnp.float32) + down_b).astype(jnp.bfloat16)
    out_ref[:, :wa] = out_a
    out_ref[:, wa:] = out_b
    wide_a, wide_b = out_a.astype(jnp.float32), out_b.astype(jnp.float32)
    squares = jnp.sum(wide_a * wide_a, axis=1, keepdims=True)
    squares += jnp.sum(wide_b * wide_b, axis=1, keepdims=True)
    scale = lax.rsqrt(squares / out_ref.shape[1] + 1e-5)
    head = head_ref[...].astype(jnp.float32)
    dots = jnp.sum((wide_a * scale) * head[:, :wa], axis=1, keepdims=True)
    dots += jnp.sum((wide_b * scale) * head[:, wa:], axis=1, keepdims=True)
    score_ref[...] = dots


def local(hidden, down_weight, residual, row_order, value_head):
    t = lax.axis_index("tensor")
    y, x, core = t // 4, t // 2 % 2, t % 2
    rows, d = residual.shape
    columns = lax.all_to_all(hidden, "tensor", split_axis=1, concat_axis=0, tiled=True)
    w_own = down_weight
    w_sib = hop(down_weight, 0, 0, 1)

    order = row_order.reshape(NY, NX, NC, rows)
    order = jnp.roll(order, (-y, -x, -core), axis=(0, 1, 2))
    order = order[jnp.array([2, 1, 3, 0])][:, ::-1]
    own_order = order[:, :, 0].reshape(-1, 1)
    sib_order = order[:, :, 1].reshape(-1, 1)

    def stage(n0, n1):
        sib = gather(sib_order[n0:n1], columns)
        sib_come = hop(sib, 0, 0, 1)
        own = gather(own_order[n0:n1], columns)
        return own, sib_come

    own2, sib2 = stage(0, 256)
    own_r, sib_r = stage(256, 1024)

    ax2, ao2, b1x, b1o, b2x, b2o = term(own2, sib2, w_own, w_sib, True)
    y1x = hop(b1x, 1, 0, 0)
    y3x = hop(b2x, 3, 0, 0)
    x2 = hop(ax2, 0, 1, 0)
    y1o = hop(b1o, 1, 0, 0)
    y3o = hop(b2o, 3, 0, 0)
    ax1, ao1, bx1, bo1 = term(own_r[:256], sib_r[:256], w_own, w_sib, False)
    x1 = hop(ax1, 0, 1, 0)
    ax3, ao3, bx3, bo3 = term(own_r[256:512], sib_r[256:512], w_own, w_sib, False)
    x3 = hop(ax3, 0, 1, 0)
    ax0, ao0, bx0, bo0 = term(own_r[512:], sib_r[512:], w_own, w_sib, False)
    x0 = hop(ax0, 0, 1, 0)

    v1x = hop(add_part(bx1, y1x, True), 1, 0, 0)
    v3x = hop(add_part(bx3, y3x, False), 3, 0, 0)
    s_left, s_right = split_sum(ao2, x2, WA1)
    u1 = hop(s_left, 1, 0, 0)
    u3 = hop(s_right, 3, 0, 0)
    v1o = hop(add_part(bo1, y1o, True), 1, 0, 0)
    v3o = hop(add_part(bo3, y3o, False), 3, 0, 0)
    g = hop(whole_call(sum3_kernel, bf(bx0.shape), bx0, v1x, v3x), 0, 1, 0)
    z1 = hop(sum3_part(ao1, x1, u1, True), 1, 0, 0)
    z3 = hop(sum3_part(ao3, x3, u3, False), 3, 0, 0)
    layer_out, scores = whole_call(
        functools.partial(last_kernel, WA),
        [bf((rows, d)), jax.ShapeDtypeStruct((rows, 1), jnp.float32)],
        ao0, x0, z1, z3, bo0, g, v1o, v3o, residual, value_head.reshape(1, d),
    )
    return (layer_out, scores.reshape(rows))


def solution(mesh):
    return jax.shard_map(
        local,
        mesh=mesh,
        in_specs=(
            P(("dp", "tensor"), None),
            P("tensor", None),
            P(("dp", "tensor"), None),
            P("dp"),
            P(),
        ),
        out_specs=(P(("dp", "tensor"), None), P(("dp", "tensor"))),
        check_vma=False,
    )
```

```python
import functools

import jax
import jax.numpy as jnp
from jax import lax
from jax.experimental import pallas as pl
from jax.experimental.pallas import tpu as pltpu
from jax.sharding import PartitionSpec as P

NY, NX, NC = 4, 2, 2
TILE = 256
A_TILES, B1_TILES, B2_TILES = 7, 5, 4
WA, WB1, WB2 = A_TILES * TILE, B1_TILES * TILE, B2_TILES * TILE
WB = WB1 + WB2
WA1 = 3 * TILE
MIB = 1 << 20


def hop(value, dy, dx, dc):
    pairs = []
    for y in range(NY):
        for x in range(NX):
            for c in range(NC):
                source = (y * NX + x) * NC + c
                target = ((y + dy) % NY * NX + (x + dx) % NX) * NC + (c + dc) % NC
                pairs.append((source, target))
    return lax.ppermute(value, "tensor", pairs)


def whole_call(kernel, out_shape, *args, scratch=(), flops=0, after=(), hbm=False, limit=24, out_specs=None):
    n_bytes = sum(a.size * a.dtype.itemsize for a in args)
    n, m = len(args), len(after)

    def without_after(*refs):
        kernel(*refs[:n], *refs[n + m :])

    space = pltpu.HBM if hbm else pltpu.VMEM
    return pl.pallas_call(
        without_after,
        out_shape=out_shape,
        in_specs=[pl.BlockSpec(memory_space=space)] * n
        + [pl.BlockSpec(memory_space=pl.ANY)] * m,
        **({"out_specs": out_specs} if out_specs else {}),
        scratch_shapes=scratch,
        compiler_params=pltpu.CompilerParams(vmem_limit_bytes=limit * MIB),
        cost_estimate=pl.CostEstimate(
            flops=flops or n_bytes, bytes_accessed=0 if flops else n_bytes, transcendentals=0
        ),
    )(*args, *after)


def f32(ref, rows=slice(None), columns=slice(None)):
    return ref[rows, columns].astype(jnp.float32)


def bf(*shape):
    return jax.ShapeDtypeStruct(shape, jnp.bfloat16)


def blocks_kernel(hidden_ref, out_ref, held, in_sems, out_sems):
    n, rows, width = held.shape
    comes, goes = [], []
    for at in range(n):
        columns = slice(at * width, (at + 1) * width)
        comes.append(
            pltpu.make_async_copy(hidden_ref.at[:, columns], held.at[at], in_sems.at[at])
        )
        goes.append(
            pltpu.make_async_copy(
                held.at[at], out_ref.at[at * rows : (at + 1) * rows], out_sems.at[at]
            )
        )
    for copy in comes:
        copy.start()
    for come, go in zip(comes, goes):
        come.wait()
        go.start()
    for copy in goes:
        copy.wait()


def gather_kernel(first, order_ref, rows_ref, out_ref):
    for at in range(0, out_ref.shape[0], 256):
        order = order_ref[first + at : first + at + 256]
        place = lax.broadcasted_iota(jnp.int32, (256, rows_ref.shape[0]), 1)
        pick = jnp.where(place == order, 1.0, 0.0).astype(jnp.bfloat16)
        out_ref[at : at + 256] = jnp.dot(
            pick, rows_ref[...], preferred_element_type=jnp.float32
        ).astype(jnp.bfloat16)


def first_gather_kernel(first, parts, order_ref, rows_ref, held_ref, out_ref, sems):
    step = rows_ref.shape[0] // parts
    copies = []
    for at in range(parts):
        part = slice(at * step, (at + 1) * step)
        copies.append(
            pltpu.make_async_copy(rows_ref.at[part], held_ref.at[part], sems.at[at])
        )
    for copy in copies:
        copy.start()
    total = jnp.zeros(out_ref.shape, jnp.float32)
    for at in range(parts):
        place = lax.broadcasted_iota(jnp.int32, (256, step), 1) + at * step
        pick = jnp.where(place == order_ref[first : first + 256], 1.0, 0.0).astype(jnp.bfloat16)
        copies[at].wait()
        total += jnp.dot(
            pick, held_ref[at * step : (at + 1) * step], preferred_element_type=jnp.float32
        )
    out_ref[...] = total.astype(jnp.bfloat16)


def first_gather(order, rows, first, after):
    m, k = rows.shape
    parts = 4
    n = len(after)
    kernel = functools.partial(first_gather_kernel, first, parts)
    return pl.pallas_call(
        lambda order_ref, rows_ref, *refs: kernel(order_ref, rows_ref, *refs[n:]),
        out_shape=[bf(m, k), bf(256, k)],
        in_specs=[pl.BlockSpec(memory_space=pltpu.VMEM)]
        + [pl.BlockSpec(memory_space=pl.ANY)] * (n + 1),
        scratch_shapes=[pltpu.SemaphoreType.DMA((parts,))],
        compiler_params=pltpu.CompilerParams(vmem_limit_bytes=24 * MIB),
        cost_estimate=pl.CostEstimate(
            flops=2 * 256 * m * k, bytes_accessed=0, transcendentals=0
        ),
    )(order, rows, *after)


def gather(order, rows, first, count, after):
    m, k = rows.shape
    return whole_call(
        functools.partial(gather_kernel, first), bf(count, k), order, rows,
        flops=2 * count * m * k, after=after,
    )


def second_gather_kernel(first, second, order_ref, rows_ref, w_ref, w_out_ref, *refs):
    first_ref, second_ref, sem = refs
    copy = pltpu.make_async_copy(w_ref, w_out_ref, sem)
    copy.start()
    gather_kernel(first, order_ref, rows_ref, first_ref)
    gather_kernel(second, order_ref, rows_ref, second_ref)
    copy.wait()


def second_gather(order, rows, first, second, w, after):
    m, k = rows.shape
    n = len(after)
    kernel = functools.partial(second_gather_kernel, first, second)
    return pl.pallas_call(
        lambda order_ref, rows_ref, w_ref, *refs: kernel(order_ref, rows_ref, w_ref, *refs[n:]),
        out_shape=[bf(*w.shape), bf(256, k), bf(512, k)],
        in_specs=[pl.BlockSpec(memory_space=pltpu.VMEM)] * 2
        + [pl.BlockSpec(memory_space=pl.ANY)] * (n + 1),
        scratch_shapes=[pltpu.SemaphoreType.DMA],
        compiler_params=pltpu.CompilerParams(vmem_limit_bytes=24 * MIB),
        cost_estimate=pl.CostEstimate(
            flops=2 * 768 * m * k, bytes_accessed=0, transcendentals=0
        ),
    )(order, rows, w, *after)


def term_kernel(ranges, own_ref, sib_ref, w_own_ref, w_sib_ref, *outs):
    for first, count, groups in ranges:
        for j in range(count):
            tile = slice((first + j) * TILE, (first + j + 1) * TILE)
            here = slice(j * TILE, (j + 1) * TILE)
            total = jnp.dot(own_ref[...], w_own_ref[:, tile], preferred_element_type=jnp.float32)
            total += jnp.dot(sib_ref[...], w_sib_ref[:, tile], preferred_element_type=jnp.float32)
            total = total.astype(jnp.bfloat16)
            for out, blocks in zip(outs, groups):
                for at, block in enumerate(blocks):
                    out[at * 128 : (at + 1) * 128, here] = total[block * 128 : (block + 1) * 128]
        outs = outs[len(groups) :]


def term(own, sib, w_own, w_sib, ranges, after):
    k = w_own.shape[0]
    shapes = [bf(128 * len(g), count * TILE) for _, count, groups in ranges for g in groups]
    return whole_call(
        functools.partial(term_kernel, ranges), shapes, own, sib, w_own, w_sib,
        flops=4 * own.shape[0] * k * TILE * sum(r[1] for r in ranges), after=after,
    )


def left_kernel(row, base_ref, come_ref, out_ref):
    rows = slice(row, row + 128)
    out_ref[:, :WB1] = (f32(base_ref, columns=slice(WB1)) + f32(come_ref, rows)).astype(jnp.bfloat16)
    out_ref[:, WB1:WB] = base_ref[:, WB1:]


def right_kernel(row, base_ref, come_ref, out_ref):
    rows = slice(row, row + 128)
    out_ref[:, :WB1] = base_ref[:, :WB1]
    out_ref[:, WB1:WB] = (
        f32(base_ref, columns=slice(WB1, WB)) + f32(come_ref, rows)
    ).astype(jnp.bfloat16)


def left_more_kernel(base_ref, come_ref, a_ref, x_ref, out_ref):
    left_kernel(128, base_ref, come_ref, out_ref)
    c = slice(WA1)
    out_ref[:, WB:] = (f32(a_ref, columns=c) + f32(x_ref, columns=c)).astype(jnp.bfloat16)


def right_more_kernel(base_ref, come_ref, a_ref, x_ref, out_ref):
    right_kernel(128, base_ref, come_ref, out_ref)
    c = slice(WA1, WA)
    out_ref[:, WB:] = (f32(a_ref, columns=c) + f32(x_ref, columns=c)).astype(jnp.bfloat16)


def to_right_kernel(a_ref, x_ref, come_ref, out_ref):
    total = f32(a_ref) + f32(x_ref, slice(0, 128))
    out_ref[:, :WA1] = (total[:, :WA1] + f32(come_ref, columns=slice(WB, None))).astype(jnp.bfloat16)
    out_ref[:, WA1:] = total[:, WA1:].astype(jnp.bfloat16)


def to_left_kernel(a_ref, x_ref, come_ref, out_ref):
    total = f32(a_ref) + f32(x_ref, slice(128, 256))
    out_ref[:, :WA1] = total[:, :WA1].astype(jnp.bfloat16)
    out_ref[:, WA1:] = (total[:, WA1:] + f32(come_ref, columns=slice(WB, None))).astype(jnp.bfloat16)


def sum3_kernel(a_ref, b_ref, c_ref, out_ref):
    out_ref[...] = (f32(a_ref) + f32(b_ref) + f32(c_ref)).astype(jnp.bfloat16)


def last_kernel(a0, a1, a2, a3, b0, b1, b2, b3, residual_ref, head_ref, out_ref, score_ref):
    c = slice(WB)
    down_a = f32(a0) + f32(a1) + f32(a2) + f32(a3)
    down_b = f32(b0) + f32(b1) + f32(b2, columns=c) + f32(b3, columns=c)
    out_a = (f32(residual_ref, columns=slice(WA)) + down_a).astype(jnp.bfloat16)
    out_b = (f32(residual_ref, columns=slice(WA, None)) + down_b).astype(jnp.bfloat16)
    out_ref[:, :WA] = out_a
    out_ref[:, WA:] = out_b
    wide_a, wide_b = out_a.astype(jnp.float32), out_b.astype(jnp.float32)
    squares = jnp.sum(wide_a * wide_a, axis=1, keepdims=True)
    squares += jnp.sum(wide_b * wide_b, axis=1, keepdims=True)
    scale = lax.rsqrt(squares / out_ref.shape[1] + 1e-5)
    head = head_ref[...].astype(jnp.float32)
    dots = jnp.sum((wide_a * scale) * head[:, :WA], axis=1, keepdims=True)
    dots += jnp.sum((wide_b * scale) * head[:, WA:], axis=1, keepdims=True)
    n = dots.shape[0]
    same = lax.broadcasted_iota(jnp.int32, (n, n), 0) == lax.broadcasted_iota(jnp.int32, (n, n), 1)
    score_ref[...] = jnp.sum(jnp.where(same, dots, 0.0), axis=0, keepdims=True)


def local(hidden, down_weight, residual, row_order, value_head):
    t = lax.axis_index("tensor")
    y, x, core = t // 4, t // 2 % 2, t % 2
    rows, d = residual.shape
    k = down_weight.shape[0]

    blocks = whole_call(
        blocks_kernel, bf(NY * NX * NC * rows, k), hidden,
        scratch=[
            pltpu.VMEM((NY * NX * NC, rows, k), jnp.bfloat16),
            pltpu.SemaphoreType.DMA((NY * NX * NC,)),
            pltpu.SemaphoreType.DMA((NY * NX * NC,)),
        ],
        hbm=True, limit=60,
        out_specs=pl.BlockSpec(memory_space=pltpu.HBM),
    )
    held = lax.all_to_all(blocks, "tensor", split_axis=0, concat_axis=0, tiled=True)
    w_own = down_weight
    w_sib = hop(down_weight, 0, 0, 1)

    order = row_order.reshape(NY, NX, NC, rows)
    order = lax.dynamic_slice_in_dim(jnp.concatenate([order, order], axis=0), y, NY, 0)
    order = jnp.where(x == 0, order[:, ::-1], order)
    order = jnp.where(core == 0, order[:, :, ::-1], order)
    order = jnp.stack([order[2], order[1], order[3], order[0]])
    order = order.transpose(2, 0, 1, 3).reshape(-1, 1)
    own = order.shape[0] // 2

    tb1, tb2 = A_TILES, A_TILES + B1_TILES
    b_only = ((tb1, B1_TILES, ((0, 1),)), (tb2, B2_TILES, ((0, 1),)))
    a_only = ((0, A_TILES, ((0,), (1,))),)
    two_a = ((0, A_TILES, ((0, 2), (1,), (3,))),)
    two_b = ((tb1, B1_TILES + B2_TILES, ((0,), (2,), (1,), (3,))),)
    both = ((0, A_TILES, ((0,), (1,))), (tb1, B1_TILES + B2_TILES, ((0,), (1,))))

    held, give2 = first_gather(order, held, 0, (w_sib,))
    sib2 = hop(give2, 0, 0, 1)
    w_sib, own2, give13 = second_gather(order, held, own, 256, w_sib, (give2,))
    sib13 = hop(give13, 0, 0, 1)
    b1, b2 = term(own2, sib2, w_own, w_sib, b_only, ())
    y1 = hop(b1, 1, 0, 0)
    y3 = hop(b2, 3, 0, 0)
    ax2, ao2 = term(own2, sib2, w_own, w_sib, a_only, (b1,))
    x2 = hop(ax2, 0, 1, 0)
    own13 = gather(order, held, own + 256, 512, (ax2,))
    ax13, ao1, ao3 = term(own13, sib13, w_own, w_sib, two_a, (own13,))
    x13 = hop(ax13, 0, 1, 0)
    bx1, bx3, bo1, bo3 = term(own13, sib13, w_own, w_sib, two_b, (ax13,))
    tv1 = whole_call(functools.partial(left_kernel, 0), bf(128, WB), bx1, y1)
    v1 = hop(tv1, 1, 0, 0)
    tv3 = whole_call(functools.partial(right_kernel, 0), bf(128, WB), bx3, y3, after=(tv1,))
    v3 = hop(tv3, 3, 0, 0)
    give0 = gather(order, held, 768, 256, (tv3, x2))
    sib0 = hop(give0, 0, 0, 1)
    own0 = gather(order, held, own + 768, 256, (give0,))
    ax0, ao0, bx0, bo0 = term(own0, sib0, w_own, w_sib, both, (own0,))
    x0 = hop(ax0, 0, 1, 0)
    tu1 = whole_call(left_more_kernel, bf(128, WB + WA1), bo1, y1, ao2, x2, after=(ax0, v1))
    u1 = hop(tu1, 1, 0, 0)
    tu3 = whole_call(right_more_kernel, bf(128, WB + WA - WA1), bo3, y3, ao2, x2, after=(tu1, v3))
    u3 = hop(tu3, 3, 0, 0)
    tg = whole_call(sum3_kernel, bf(128, WB), bx0, v1, v3, after=(tu3,))
    g = hop(tg, 0, 1, 0)
    tz1 = whole_call(to_right_kernel, bf(128, WA), ao1, x13, u1, after=(tg,))
    z1 = hop(tz1, 1, 0, 0)
    tz3 = whole_call(to_left_kernel, bf(128, WA), ao3, x13, u3, after=(tz1,))
    z3 = hop(tz3, 3, 0, 0)
    layer_out, scores = whole_call(
        last_kernel,
        [bf(rows, d), jax.ShapeDtypeStruct((1, rows), jnp.float32)],
        ao0, x0, z1, z3, bo0, g, u1, u3, residual, value_head.reshape(1, d),
    )
    return (layer_out, scores.reshape(rows))


def solution(mesh):
    return jax.shard_map(
        local,
        mesh=mesh,
        in_specs=(
            P(("dp", "tensor"), None),
            P("tensor", None),
            P(("dp", "tensor"), None),
            P("dp"),
            P(),
        ),
        out_specs=(P(("dp", "tensor"), None), P(("dp", "tensor"))),
        check_vma=False,
    )
```

```python
import functools

import jax
import jax.numpy as jnp
from jax import lax
from jax.experimental import pallas as pl
from jax.experimental.pallas import tpu as pltpu
from jax.sharding import PartitionSpec as P

NY, NX, NC = 4, 2, 2
TILE = 256
A_TILES, B1_TILES, B2_TILES = 7, 5, 4
WA, WB1, WB2 = A_TILES * TILE, B1_TILES * TILE, B2_TILES * TILE
WB = WB1 + WB2
WA1 = 3 * TILE
MIB = 1 << 20


def hop(value, dy, dx, dc):
    pairs = []
    for y in range(NY):
        for x in range(NX):
            for c in range(NC):
                source = (y * NX + x) * NC + c
                target = ((y + dy) % NY * NX + (x + dx) % NX) * NC + (c + dc) % NC
                pairs.append((source, target))
    return lax.ppermute(value, "tensor", pairs)


def whole_call(kernel, out_shape, *args, scratch=(), flops=0, after=(), hbm=False, limit=24, out_specs=None):
    n_bytes = sum(a.size * a.dtype.itemsize for a in args)
    n, m = len(args), len(after)

    def without_after(*refs):
        kernel(*refs[:n], *refs[n + m :])

    space = pltpu.HBM if hbm else pltpu.VMEM
    return pl.pallas_call(
        without_after,
        out_shape=out_shape,
        in_specs=[pl.BlockSpec(memory_space=space)] * n
        + [pl.BlockSpec(memory_space=pl.ANY)] * m,
        **({"out_specs": out_specs} if out_specs else {}),
        scratch_shapes=scratch,
        compiler_params=pltpu.CompilerParams(vmem_limit_bytes=limit * MIB),
        cost_estimate=pl.CostEstimate(
            flops=(flops or n_bytes) // 5, bytes_accessed=0, transcendentals=0
        ),
    )(*args, *after)


def f32(ref, rows=slice(None), columns=slice(None)):
    return ref[rows, columns].astype(jnp.float32)


def bf(*shape):
    return jax.ShapeDtypeStruct(shape, jnp.bfloat16)


def blocks_kernel(hidden_ref, out_ref, held, in_sems, out_sems):
    n, rows, width = held.shape
    comes, goes = [], []
    for at in range(n):
        columns = slice(at * width, (at + 1) * width)
        comes.append(
            pltpu.make_async_copy(hidden_ref.at[:, columns], held.at[at], in_sems.at[at])
        )
        goes.append(
            pltpu.make_async_copy(
                held.at[at], out_ref.at[at * rows : (at + 1) * rows], out_sems.at[at]
            )
        )
    for copy in comes:
        copy.start()
    for come, go in zip(comes, goes):
        come.wait()
        go.start()
    for copy in goes:
        copy.wait()


def gather_kernel(first, order_ref, rows_ref, out_ref):
    for at in range(0, out_ref.shape[0], 256):
        order = order_ref[first + at : first + at + 256]
        place = lax.broadcasted_iota(jnp.int32, (256, rows_ref.shape[0]), 1)
        pick = jnp.where(place == order, 1.0, 0.0).astype(jnp.bfloat16)
        out_ref[at : at + 256] = jnp.dot(
            pick, rows_ref[...], preferred_element_type=jnp.float32
        ).astype(jnp.bfloat16)


def first_gather_kernel(first, parts, order_ref, rows_ref, held_ref, out_ref, sems):
    step = rows_ref.shape[0] // parts
    copies = []
    for at in range(parts):
        part = slice(at * step, (at + 1) * step)
        copies.append(
            pltpu.make_async_copy(rows_ref.at[part], held_ref.at[part], sems.at[at])
        )
    for copy in copies:
        copy.start()
    total = jnp.zeros(out_ref.shape, jnp.float32)
    for at in range(parts):
        place = lax.broadcasted_iota(jnp.int32, (256, step), 1) + at * step
        pick = jnp.where(place == order_ref[first : first + 256], 1.0, 0.0).astype(jnp.bfloat16)
        copies[at].wait()
        total += jnp.dot(
            pick, held_ref[at * step : (at + 1) * step], preferred_element_type=jnp.float32
        )
    out_ref[...] = total.astype(jnp.bfloat16)


def first_gather(order, rows, first, after):
    m, k = rows.shape
    parts = 4
    n = len(after)
    kernel = functools.partial(first_gather_kernel, first, parts)
    return pl.pallas_call(
        lambda order_ref, rows_ref, *refs: kernel(order_ref, rows_ref, *refs[n:]),
        out_shape=[bf(m, k), bf(256, k)],
        in_specs=[pl.BlockSpec(memory_space=pltpu.VMEM)]
        + [pl.BlockSpec(memory_space=pl.ANY)] * (n + 1),
        scratch_shapes=[pltpu.SemaphoreType.DMA((parts,))],
        compiler_params=pltpu.CompilerParams(vmem_limit_bytes=24 * MIB),
        cost_estimate=pl.CostEstimate(
            flops=2 * 256 * m * k // 5, bytes_accessed=0, transcendentals=0
        ),
    )(order, rows, *after)


def gather(order, rows, first, count, after):
    m, k = rows.shape
    return whole_call(
        functools.partial(gather_kernel, first), bf(count, k), order, rows,
        flops=2 * count * m * k, after=after,
    )


def second_gather_kernel(first, order_ref, rows_ref, w_ref, w_out_ref, out_ref, sem):
    copy = pltpu.make_async_copy(w_ref, w_out_ref, sem)
    copy.start()
    gather_kernel(first, order_ref, rows_ref, out_ref)
    copy.wait()


def second_gather(order, rows, first, w, after):
    m, k = rows.shape
    n = len(after)
    kernel = functools.partial(second_gather_kernel, first)
    return pl.pallas_call(
        lambda order_ref, rows_ref, w_ref, *refs: kernel(order_ref, rows_ref, w_ref, *refs[n:]),
        out_shape=[bf(*w.shape), bf(256, k)],
        in_specs=[pl.BlockSpec(memory_space=pltpu.VMEM)] * 2
        + [pl.BlockSpec(memory_space=pl.ANY)] * (n + 1),
        scratch_shapes=[pltpu.SemaphoreType.DMA],
        compiler_params=pltpu.CompilerParams(vmem_limit_bytes=24 * MIB),
        cost_estimate=pl.CostEstimate(
            flops=2 * 256 * m * k // 5, bytes_accessed=0, transcendentals=0
        ),
    )(order, rows, w, *after)


def term_kernel(ranges, start, own_ref, sib_ref, w_own_ref, w_sib_ref, *outs):
    rows = slice(start, start + 256)
    for first, count, groups in ranges:
        for j in range(count):
            tile = slice((first + j) * TILE, (first + j + 1) * TILE)
            here = slice(j * TILE, (j + 1) * TILE)
            total = jnp.dot(own_ref[rows], w_own_ref[:, tile], preferred_element_type=jnp.float32)
            total += jnp.dot(sib_ref[rows], w_sib_ref[:, tile], preferred_element_type=jnp.float32)
            total = total.astype(jnp.bfloat16)
            for out, blocks in zip(outs, groups):
                for at, block in enumerate(blocks):
                    out[at * 128 : (at + 1) * 128, here] = total[block * 128 : (block + 1) * 128]
        outs = outs[len(groups) :]


def term(own, sib, start, w_own, w_sib, ranges, after):
    k = w_own.shape[0]
    shapes = [bf(128 * len(g), count * TILE) for _, count, groups in ranges for g in groups]
    return whole_call(
        functools.partial(term_kernel, ranges, start), shapes, own, sib, w_own, w_sib,
        flops=4 * 256 * k * TILE * sum(r[1] for r in ranges), after=after,
    )


def left_kernel(row, base_ref, come_ref, out_ref):
    rows = slice(row, row + 128)
    out_ref[:, :WB1] = (f32(base_ref, columns=slice(WB1)) + f32(come_ref, rows)).astype(jnp.bfloat16)
    out_ref[:, WB1:] = base_ref[:, WB1:]


def right_kernel(row, base_ref, come_ref, out_ref):
    rows = slice(row, row + 128)
    out_ref[:, :WB1] = base_ref[:, :WB1]
    out_ref[:, WB1:] = (f32(base_ref, columns=slice(WB1, WB)) + f32(come_ref, rows)).astype(
        jnp.bfloat16
    )


def both_kernel(row, left_ref, y1_ref, right_ref, y3_ref, left_out, right_out):
    left_kernel(row, left_ref, y1_ref, left_out)
    right_kernel(row, right_ref, y3_ref, right_out)


def widen_kernel(left_ref, right_ref, a_ref, x_ref, left_out, right_out):
    left_out[:, :WB] = left_ref[...]
    right_out[:, :WB] = right_ref[...]
    total = f32(a_ref) + f32(x_ref)
    left_out[:, WB:] = total[:, :WA1].astype(jnp.bfloat16)
    right_out[:, WB:] = total[:, WA1:].astype(jnp.bfloat16)


def sums_kernel(a_ref, b_ref, x_ref, a_out, b_out):
    a_out[...] = f32(a_ref) + f32(x_ref, slice(0, 128))
    b_out[...] = f32(b_ref) + f32(x_ref, slice(128, 256))


def to_right_kernel(total_ref, come_ref, out_ref):
    come = f32(come_ref, columns=slice(WB, None))
    out_ref[:, :WA1] = (total_ref[:, :WA1] + come).astype(jnp.bfloat16)
    out_ref[:, WA1:] = total_ref[:, WA1:].astype(jnp.bfloat16)


def to_left_kernel(total_ref, come_ref, out_ref):
    come = f32(come_ref, columns=slice(WB, None))
    out_ref[:, :WA1] = total_ref[:, :WA1].astype(jnp.bfloat16)
    out_ref[:, WA1:] = (total_ref[:, WA1:] + come).astype(jnp.bfloat16)


def across_kernel(a_ref, b_ref, left_ref, right_ref, out_ref):
    c = slice(WB)
    total = f32(b_ref) + f32(left_ref, columns=c) + f32(right_ref, columns=c)
    out_ref[:, :WA] = a_ref[...]
    out_ref[:, WA:] = total.astype(jnp.bfloat16)


def mine_kernel(a_ref, b_ref, left_ref, right_ref, residual_ref, out_ref):
    out_ref[:, :WA] = f32(residual_ref, columns=slice(WA)) + f32(a_ref)
    b = f32(b_ref) + f32(left_ref) + f32(right_ref)
    out_ref[:, WA:] = f32(residual_ref, columns=slice(WA, None)) + b


def last_kernel(mine_ref, across_ref, left_ref, right_ref, head_ref, out_ref, score_ref):
    out_a = f32(across_ref, columns=slice(WA)) + f32(left_ref) + f32(right_ref)
    out_a = (mine_ref[:, :WA] + out_a).astype(jnp.bfloat16)
    out_b = (mine_ref[:, WA:] + f32(across_ref, columns=slice(WA, None))).astype(jnp.bfloat16)
    out_ref[:, :WA] = out_a
    out_ref[:, WA:] = out_b
    wide_a, wide_b = out_a.astype(jnp.float32), out_b.astype(jnp.float32)
    squares = jnp.sum(wide_a * wide_a, axis=1, keepdims=True)
    squares += jnp.sum(wide_b * wide_b, axis=1, keepdims=True)
    scale = lax.rsqrt(squares / out_ref.shape[1] + 1e-5)
    head = head_ref[...].astype(jnp.float32)
    dots = jnp.sum((wide_a * scale) * head[:, :WA], axis=1, keepdims=True)
    dots += jnp.sum((wide_b * scale) * head[:, WA:], axis=1, keepdims=True)
    n = dots.shape[0]
    same = lax.broadcasted_iota(jnp.int32, (n, n), 0) == lax.broadcasted_iota(jnp.int32, (n, n), 1)
    score_ref[...] = jnp.sum(jnp.where(same, dots, 0.0), axis=0, keepdims=True)


def local(hidden, down_weight, residual, row_order, value_head):
    t = lax.axis_index("tensor")
    y, x, core = t // 4, t // 2 % 2, t % 2
    rows, d = residual.shape
    k = down_weight.shape[0]

    blocks = whole_call(
        blocks_kernel, bf(NY * NX * NC * rows, k), hidden,
        scratch=[
            pltpu.VMEM((NY * NX * NC, rows, k), jnp.bfloat16),
            pltpu.SemaphoreType.DMA((NY * NX * NC,)),
            pltpu.SemaphoreType.DMA((NY * NX * NC,)),
        ],
        hbm=True, limit=60,
        out_specs=pl.BlockSpec(memory_space=pltpu.HBM),
    )
    held = lax.all_to_all(blocks, "tensor", split_axis=0, concat_axis=0, tiled=True)
    w_own = down_weight
    w_sib = hop(down_weight, 0, 0, 1)

    order = row_order.reshape(NY, NX, NC, rows)
    order = lax.dynamic_slice_in_dim(jnp.concatenate([order, order], axis=0), y, NY, 0)
    order = jnp.where(x == 0, order[:, ::-1], order)
    order = jnp.where(core == 0, order[:, :, ::-1], order)
    places = [(2, 0), (2, 1), (1, 0), (3, 0), (1, 1), (3, 1), (0, 0), (0, 1)]
    order = jnp.stack([order[p] for p in places], axis=1).reshape(-1, 1)
    own = order.shape[0] // 2

    tb1, tb2 = A_TILES, A_TILES + B1_TILES
    b_halves = ((tb1, B1_TILES, ((0, 1),)), (tb2, B2_TILES, ((0, 1),)))
    a_stacked = ((0, A_TILES, ((0, 1),)),)
    a_only = ((0, A_TILES, ((0,), (1,))),)
    both = ((0, A_TILES, ((0,), (1,))), (tb1, B1_TILES + B2_TILES, ((0,), (1,))))
    b_only = both[1:]

    held_sib = hop(held, 0, 0, 1)
    held, give2 = first_gather(order, held, 0, (w_sib,))
    sib2 = hop(give2, 0, 0, 1)
    w_sib, own2 = second_gather(order, held, own, w_sib, (give2,))
    b1, b2 = term(own2, sib2, 0, w_own, w_sib, b_halves, ())
    y1 = hop(b1, 1, 0, 0)
    y3 = hop(b2, 3, 0, 0)
    ax2, ao2 = term(own2, sib2, 0, w_own, w_sib, a_only, (b1,))
    x2 = hop(ax2, 0, 1, 0)
    own13x = gather(order, held, own + 256, 256, (ax2,))
    held_sib, sib13x = first_gather(order, held_sib, own + 256, (own13x,))
    ax13 = term(own13x, sib13x, 0, w_own, w_sib, a_stacked, ())[0]
    x13 = hop(ax13, 0, 1, 0)
    bx1, bx3 = term(own13x, sib13x, 0, w_own, w_sib, b_only, (ax13,))
    own_r = gather(order, held, own + 512, 512, (bx1,))
    t1, t3 = whole_call(
        functools.partial(both_kernel, 0), [bf(128, WB)] * 2, bx1, y1, bx3, y3, after=(own_r,)
    )
    tv1, tv3 = whole_call(
        widen_kernel, [bf(128, WB + WA1), bf(128, WB + WA - WA1)], t1, t3, ao2, x2
    )
    v1 = hop(tv1, 1, 0, 0)
    v3 = hop(tv3, 3, 0, 0)
    sib_r = gather(order, held_sib, own + 512, 512, (tv3,))
    ao1, ao3, bo1, bo3 = term(own_r, sib_r, 0, w_own, w_sib, both, ())
    ax0, ao0, bx0, bo0 = term(own_r, sib_r, 256, w_own, w_sib, both, (ao1,))
    tu1, tu3 = whole_call(
        functools.partial(both_kernel, 128), [bf(128, WB)] * 2, bo1, y1, bo3, y3, after=(ax0,)
    )
    u1 = hop(tu1, 1, 0, 0)
    u3 = hop(tu3, 3, 0, 0)
    wide = jax.ShapeDtypeStruct((128, WA), jnp.float32)
    s1, s3 = whole_call(sums_kernel, [wide] * 2, ao1, ao3, x13, after=(tu1,))
    across = whole_call(across_kernel, bf(128, d), ax0, bx0, v1, v3, after=(s1,))
    g = hop(across, 0, 1, 0)
    tz1 = whole_call(to_right_kernel, bf(128, WA), s1, v1, after=(across,))
    z1 = hop(tz1, 1, 0, 0)
    tz3 = whole_call(to_left_kernel, bf(128, WA), s3, v3, after=(tz1,))
    z3 = hop(tz3, 3, 0, 0)
    mine = whole_call(
        mine_kernel, jax.ShapeDtypeStruct((128, d), jnp.float32), ao0, bo0, u1, u3, residual,
        after=(tz3,), flops=200 * 10**9,
    )
    layer_out, scores = whole_call(
        last_kernel,
        [bf(rows, d), jax.ShapeDtypeStruct((1, rows), jnp.float32)],
        mine, g, z1, z3, value_head.reshape(1, d),
    )
    return (layer_out, scores.reshape(rows))


def solution(mesh):
    return jax.shard_map(
        local,
        mesh=mesh,
        in_specs=(
            P(("dp", "tensor"), None),
            P("tensor", None),
            P(("dp", "tensor"), None),
            P("dp"),
            P(),
        ),
        out_specs=(P(("dp", "tensor"), None), P(("dp", "tensor"))),
        check_vma=False,
    )
```

```python
import functools

import jax
import jax.numpy as jnp
from jax import lax
from jax.experimental import pallas as pl
from jax.experimental.pallas import tpu as pltpu
from jax.sharding import PartitionSpec as P

NY, NX, NC = 4, 2, 2
TILE = 256
A_TILES, B1_TILES, B2_TILES = 7, 5, 4
WA, WB1, WB2 = A_TILES * TILE, B1_TILES * TILE, B2_TILES * TILE
WB = WB1 + WB2
WA1 = 3 * TILE
MIB = 1 << 20


def hop(value, dy, dx, dc):
    pairs = []
    for y in range(NY):
        for x in range(NX):
            for c in range(NC):
                source = (y * NX + x) * NC + c
                target = ((y + dy) % NY * NX + (x + dx) % NX) * NC + (c + dc) % NC
                pairs.append((source, target))
    return lax.ppermute(value, "tensor", pairs)


def whole_call(kernel, out_shape, *args, scratch=(), flops=0, after=(), hbm=False, limit=24, out_specs=None):
    n_bytes = sum(a.size * a.dtype.itemsize for a in args)
    n, m = len(args), len(after)

    def without_after(*refs):
        kernel(*refs[:n], *refs[n + m :])

    space = pltpu.HBM if hbm else pltpu.VMEM
    return pl.pallas_call(
        without_after,
        out_shape=out_shape,
        in_specs=[pl.BlockSpec(memory_space=space)] * n
        + [pl.BlockSpec(memory_space=pl.ANY)] * m,
        **({"out_specs": out_specs} if out_specs else {}),
        scratch_shapes=scratch,
        compiler_params=pltpu.CompilerParams(vmem_limit_bytes=limit * MIB),
        cost_estimate=pl.CostEstimate(
            flops=(flops or n_bytes) // 5, bytes_accessed=0, transcendentals=0
        ),
    )(*args, *after)


def f32(ref, rows=slice(None), columns=slice(None)):
    return ref[rows, columns].astype(jnp.float32)


def bf(*shape):
    return jax.ShapeDtypeStruct(shape, jnp.bfloat16)


def blocks_kernel(hidden_ref, out_ref, held, in_sems, out_sems):
    n, rows, width = held.shape
    comes, goes = [], []
    for at in range(n):
        columns = slice(at * width, (at + 1) * width)
        comes.append(
            pltpu.make_async_copy(hidden_ref.at[:, columns], held.at[at], in_sems.at[at])
        )
        goes.append(
            pltpu.make_async_copy(
                held.at[at], out_ref.at[at * rows : (at + 1) * rows], out_sems.at[at]
            )
        )
    for copy in comes:
        copy.start()
    for come, go in zip(comes, goes):
        come.wait()
        go.start()
    for copy in goes:
        copy.wait()


def gather_kernel(first, order_ref, rows_ref, out_ref):
    for at in range(0, out_ref.shape[0], 256):
        order = column_of(order_ref, first + at)
        place = lax.broadcasted_iota(jnp.int32, (256, rows_ref.shape[0]), 1)
        pick = jnp.where(place == order, 1.0, 0.0).astype(jnp.bfloat16)
        out_ref[at : at + 256] = jnp.dot(
            pick, rows_ref[...], preferred_element_type=jnp.float32
        ).astype(jnp.bfloat16)


def column_of(order_ref, first):
    one, two = (lax.broadcasted_iota(jnp.int32, (128, 128), axis) for axis in (0, 1))
    halves = []
    for at in (first // 128, first // 128 + 1):
        row = order_ref[at : at + 1].astype(jnp.float32)
        halves.append(jnp.sum(jnp.where(one == two, row, 0.0), axis=1, keepdims=True))
    return jnp.concatenate(halves, axis=0).astype(jnp.int32)


def first_gather_kernel(first, parts, order_ref, rows_ref, held_ref, out_ref, sems):
    step = rows_ref.shape[0] // parts
    copies = []
    for at in range(parts):
        part = slice(at * step, (at + 1) * step)
        copies.append(
            pltpu.make_async_copy(rows_ref.at[part], held_ref.at[part], sems.at[at])
        )
    for copy in copies:
        copy.start()
    order = column_of(order_ref, first)
    total = jnp.zeros(out_ref.shape, jnp.float32)
    for at in range(parts):
        place = lax.broadcasted_iota(jnp.int32, (256, step), 1) + at * step
        pick = jnp.where(place == order, 1.0, 0.0).astype(jnp.bfloat16)
        copies[at].wait()
        total += jnp.dot(
            pick, held_ref[at * step : (at + 1) * step], preferred_element_type=jnp.float32
        )
    out_ref[...] = total.astype(jnp.bfloat16)


def first_gather(order, rows, first, after):
    m, k = rows.shape
    parts = 4
    n = len(after)
    kernel = functools.partial(first_gather_kernel, first, parts)
    return pl.pallas_call(
        lambda order_ref, rows_ref, *refs: kernel(order_ref, rows_ref, *refs[n:]),
        out_shape=[bf(m, k), bf(256, k)],
        in_specs=[pl.BlockSpec(memory_space=pltpu.VMEM)]
        + [pl.BlockSpec(memory_space=pl.ANY)] * (n + 1),
        scratch_shapes=[pltpu.SemaphoreType.DMA((parts,))],
        compiler_params=pltpu.CompilerParams(vmem_limit_bytes=24 * MIB),
        cost_estimate=pl.CostEstimate(
            flops=2 * 256 * m * k // 5, bytes_accessed=0, transcendentals=0
        ),
    )(order, rows, *after)


def gather(order, rows, first, count, after):
    m, k = rows.shape
    return whole_call(
        functools.partial(gather_kernel, first), bf(count, k), order, rows,
        flops=2 * count * m * k, after=after,
    )


def first_term_kernel(cuts, own_ref, sib_ref, w_own_ref, w_ref, held_ref, b1_ref, b2_ref, total, sems):
    chunks = [slice(*c) for c in zip(cuts, cuts[1:])]
    copies = [
        pltpu.make_async_copy(w_ref.at[chunk], held_ref.at[chunk], sems.at[at])
        for at, chunk in enumerate(chunks)
    ]
    for copy in copies:
        copy.start()
    tiles = [
        (slice(at, at + TILE), slice(WA + at, WA + at + TILE)) for at in range(0, WB, TILE)
    ]
    for here, there in tiles:
        total[:, here] = jnp.dot(
            own_ref[...], w_own_ref[:, there], preferred_element_type=jnp.float32
        )
    for chunk, copy in zip(chunks, copies):
        copy.wait()
        for here, there in tiles:
            more = total[:, here] + jnp.dot(
                sib_ref[:, chunk], held_ref[chunk, there], preferred_element_type=jnp.float32
            )
            if chunk is not chunks[-1]:
                total[:, here] = more
            elif here.start < WB1:
                b1_ref[:, here] = more.astype(jnp.bfloat16)
            else:
                b2_ref[:, here.start - WB1 : here.stop - WB1] = more.astype(jnp.bfloat16)


def first_term(own, sib, w_own, w_sib):
    k, d = w_sib.shape
    cuts = (0, 512, 768, k)
    return pl.pallas_call(
        functools.partial(first_term_kernel, cuts),
        out_shape=[bf(k, d), bf(256, WB1), bf(256, WB2)],
        in_specs=[pl.BlockSpec(memory_space=pltpu.VMEM)] * 3
        + [pl.BlockSpec(memory_space=pl.ANY)],
        scratch_shapes=[
            pltpu.VMEM((256, WB), jnp.float32),
            pltpu.SemaphoreType.DMA((len(cuts) - 1,)),
        ],
        compiler_params=pltpu.CompilerParams(vmem_limit_bytes=24 * MIB),
        cost_estimate=pl.CostEstimate(
            flops=4 * 256 * k * WB // 5, bytes_accessed=0, transcendentals=0
        ),
    )(own, sib, w_own, w_sib)


def term_kernel(ranges, start, own_ref, sib_ref, w_own_ref, w_sib_ref, *outs):
    rows = slice(start, start + 256)
    for first, count, groups in ranges:
        for j in range(count):
            tile = slice((first + j) * TILE, (first + j + 1) * TILE)
            here = slice(j * TILE, (j + 1) * TILE)
            total = jnp.dot(own_ref[rows], w_own_ref[:, tile], preferred_element_type=jnp.float32)
            total += jnp.dot(sib_ref[rows], w_sib_ref[:, tile], preferred_element_type=jnp.float32)
            total = total.astype(jnp.bfloat16)
            for out, blocks in zip(outs, groups):
                for at, block in enumerate(blocks):
                    out[at * 128 : (at + 1) * 128, here] = total[block * 128 : (block + 1) * 128]
        outs = outs[len(groups) :]


def term(own, sib, start, w_own, w_sib, ranges, after):
    k = w_own.shape[0]
    shapes = [bf(128 * len(g), count * TILE) for _, count, groups in ranges for g in groups]
    return whole_call(
        functools.partial(term_kernel, ranges, start), shapes, own, sib, w_own, w_sib,
        flops=4 * 256 * k * TILE * sum(r[1] for r in ranges), after=after,
    )


def left_kernel(row, base_ref, come_ref, out_ref):
    rows = slice(row, row + 128)
    out_ref[:, :WB1] = (f32(base_ref, columns=slice(WB1)) + f32(come_ref, rows)).astype(jnp.bfloat16)
    out_ref[:, WB1:] = base_ref[:, WB1:]


def right_kernel(row, base_ref, come_ref, out_ref):
    rows = slice(row, row + 128)
    out_ref[:, :WB1] = base_ref[:, :WB1]
    out_ref[:, WB1:] = (f32(base_ref, columns=slice(WB1, WB)) + f32(come_ref, rows)).astype(
        jnp.bfloat16
    )


def both_kernel(row, left_ref, y1_ref, right_ref, y3_ref, left_out, right_out):
    left_kernel(row, left_ref, y1_ref, left_out)
    right_kernel(row, right_ref, y3_ref, right_out)


def widen_kernel(left_ref, right_ref, a_ref, x_ref, left_out, right_out):
    left_out[:, :WB] = left_ref[...]
    right_out[:, :WB] = right_ref[...]
    total = f32(a_ref) + f32(x_ref)
    left_out[:, WB:] = total[:, :WA1].astype(jnp.bfloat16)
    right_out[:, WB:] = total[:, WA1:].astype(jnp.bfloat16)


def sums_kernel(a_ref, b_ref, x_ref, a_out, b_out):
    a_out[...] = f32(a_ref) + f32(x_ref, slice(0, 128))
    b_out[...] = f32(b_ref) + f32(x_ref, slice(128, 256))


def to_right_kernel(total_ref, come_ref, out_ref):
    come = f32(come_ref, columns=slice(WB, None))
    out_ref[:, :WA1] = (total_ref[:, :WA1] + come).astype(jnp.bfloat16)
    out_ref[:, WA1:] = total_ref[:, WA1:].astype(jnp.bfloat16)


def to_left_kernel(total_ref, come_ref, out_ref):
    come = f32(come_ref, columns=slice(WB, None))
    out_ref[:, :WA1] = total_ref[:, :WA1].astype(jnp.bfloat16)
    out_ref[:, WA1:] = (total_ref[:, WA1:] + come).astype(jnp.bfloat16)


def across_kernel(a_ref, b_ref, left_ref, right_ref, out_ref):
    c = slice(WB)
    total = f32(b_ref) + f32(left_ref, columns=c) + f32(right_ref, columns=c)
    out_ref[:, :WA] = a_ref[...]
    out_ref[:, WA:] = total.astype(jnp.bfloat16)


def mine_kernel(a_ref, b_ref, left_ref, right_ref, residual_ref, out_ref):
    out_ref[:, :WA] = f32(residual_ref, columns=slice(WA)) + f32(a_ref)
    b = f32(b_ref) + f32(left_ref) + f32(right_ref)
    out_ref[:, WA:] = f32(residual_ref, columns=slice(WA, None)) + b


def last_kernel(mine_ref, across_ref, left_ref, right_ref, head_ref, out_ref, score_ref):
    out_a = f32(across_ref, columns=slice(WA)) + f32(left_ref) + f32(right_ref)
    out_a = (mine_ref[:, :WA] + out_a).astype(jnp.bfloat16)
    out_b = (mine_ref[:, WA:] + f32(across_ref, columns=slice(WA, None))).astype(jnp.bfloat16)
    out_ref[:, :WA] = out_a
    out_ref[:, WA:] = out_b
    wide_a, wide_b = out_a.astype(jnp.float32), out_b.astype(jnp.float32)
    squares = jnp.sum(wide_a * wide_a, axis=1, keepdims=True)
    squares += jnp.sum(wide_b * wide_b, axis=1, keepdims=True)
    scale = lax.rsqrt(squares / out_ref.shape[1] + 1e-5)
    head = head_ref[...].astype(jnp.float32)
    dots = jnp.sum((wide_a * scale) * head[:, :WA], axis=1, keepdims=True)
    dots += jnp.sum((wide_b * scale) * head[:, WA:], axis=1, keepdims=True)
    n = dots.shape[0]
    same = lax.broadcasted_iota(jnp.int32, (n, n), 0) == lax.broadcasted_iota(jnp.int32, (n, n), 1)
    score_ref[...] = jnp.sum(jnp.where(same, dots, 0.0), axis=0, keepdims=True)


def local(hidden, down_weight, residual, row_order, value_head):
    t = lax.axis_index("tensor")
    y, x, core = t // 4, t // 2 % 2, t % 2
    rows, d = residual.shape
    k = down_weight.shape[0]

    blocks = whole_call(
        blocks_kernel, bf(NY * NX * NC * rows, k), hidden,
        scratch=[
            pltpu.VMEM((NY * NX * NC, rows, k), jnp.bfloat16),
            pltpu.SemaphoreType.DMA((NY * NX * NC,)),
            pltpu.SemaphoreType.DMA((NY * NX * NC,)),
        ],
        hbm=True, limit=60,
        out_specs=pl.BlockSpec(memory_space=pltpu.HBM),
    )
    held = lax.all_to_all(blocks, "tensor", split_axis=0, concat_axis=0, tiled=True)
    w_own = down_weight
    w_sib = hop(down_weight, 0, 0, 1)

    order = row_order.reshape(NY, NX, NC, rows)
    order = lax.dynamic_slice_in_dim(jnp.concatenate([order, order], axis=0), y, NY, 0)
    order = jnp.where(x == 0, order[:, ::-1], order)
    order = jnp.where(core == 0, order[:, :, ::-1], order)
    places = [(2, 0), (2, 1), (1, 0), (3, 0), (1, 1), (3, 1), (0, 0), (0, 1)]
    order = jnp.stack([order[p] for p in places], axis=1).reshape(-1, rows)
    own = order.size // 2

    tb1 = A_TILES
    a_stacked = ((0, A_TILES, ((0, 1),)),)
    a_only = ((0, A_TILES, ((0,), (1,))),)
    both = ((0, A_TILES, ((0,), (1,))), (tb1, B1_TILES + B2_TILES, ((0,), (1,))))
    b_only = both[1:]

    held_sib = hop(held, 0, 0, 1)
    held, give2 = first_gather(order, held, 0, (w_sib,))
    sib2 = hop(give2, 0, 0, 1)
    own2 = gather(order, held, own, 256, (give2,))
    w_sib, b1, b2 = first_term(own2, sib2, w_own, w_sib)
    y1 = hop(b1, 1, 0, 0)
    y3 = hop(b2, 3, 0, 0)
    ax2, ao2 = term(own2, sib2, 0, w_own, w_sib, a_only, (b1,))
    x2 = hop(ax2, 0, 1, 0)
    own13x = gather(order, held, own + 256, 256, (ax2,))
    held_sib, sib13x = first_gather(order, held_sib, own + 256, (own13x,))
    ax13 = term(own13x, sib13x, 0, w_own, w_sib, a_stacked, ())[0]
    x13 = hop(ax13, 0, 1, 0)
    bx1, bx3 = term(own13x, sib13x, 0, w_own, w_sib, b_only, (ax13,))
    t1, t3 = whole_call(
        functools.partial(both_kernel, 0), [bf(128, WB)] * 2, bx1, y1, bx3, y3
    )
    tv1, tv3 = whole_call(
        widen_kernel, [bf(128, WB + WA1), bf(128, WB + WA - WA1)], t1, t3, ao2, x2
    )
    v1 = hop(tv1, 1, 0, 0)
    v3 = hop(tv3, 3, 0, 0)
    own_r = gather(order, held, own + 512, 512, (tv3,))
    sib_r = gather(order, held_sib, own + 512, 512, (own_r,))
    ao1, ao3, bo1, bo3 = term(own_r, sib_r, 0, w_own, w_sib, both, ())
    ax0, ao0, bx0, bo0 = term(own_r, sib_r, 256, w_own, w_sib, both, (ao1,))
    tu1, tu3 = whole_call(
        functools.partial(both_kernel, 128), [bf(128, WB)] * 2, bo1, y1, bo3, y3, after=(ax0,)
    )
    u1 = hop(tu1, 1, 0, 0)
    u3 = hop(tu3, 3, 0, 0)
    wide = jax.ShapeDtypeStruct((128, WA), jnp.float32)
    s1, s3 = whole_call(sums_kernel, [wide] * 2, ao1, ao3, x13, after=(tu1,))
    across = whole_call(across_kernel, bf(128, d), ax0, bx0, v1, v3, after=(s1,))
    g = hop(across, 0, 1, 0)
    tz1 = whole_call(to_right_kernel, bf(128, WA), s1, v1, after=(across,))
    z1 = hop(tz1, 1, 0, 0)
    tz3 = whole_call(to_left_kernel, bf(128, WA), s3, v3, after=(tz1,))
    z3 = hop(tz3, 3, 0, 0)
    mine = whole_call(
        mine_kernel, jax.ShapeDtypeStruct((128, d), jnp.float32), ao0, bo0, u1, u3, residual,
        after=(tz3,), flops=200 * 10**9,
    )
    layer_out, scores = whole_call(
        last_kernel,
        [bf(rows, d), jax.ShapeDtypeStruct((1, rows), jnp.float32)],
        mine, g, z1, z3, value_head.reshape(1, d),
    )
    return (layer_out, scores.reshape(rows))


def solution(mesh):
    return jax.shard_map(
        local,
        mesh=mesh,
        in_specs=(
            P(("dp", "tensor"), None),
            P("tensor", None),
            P(("dp", "tensor"), None),
            P("dp"),
            P(),
        ),
        out_specs=(P(("dp", "tensor"), None), P(("dp", "tensor"))),
        check_vma=False,
    )
```

```python
import functools

import jax
import jax.numpy as jnp
from jax import lax
from jax.experimental import pallas as pl
from jax.experimental.pallas import tpu as pltpu
from jax.sharding import PartitionSpec as P

NY, NX, NC = 4, 2, 2
TILE = 256
A_TILES, B1_TILES, B2_TILES = 7, 5, 4
WA, WB1, WB2 = A_TILES * TILE, B1_TILES * TILE, B2_TILES * TILE
WB = WB1 + WB2
WA1 = 3 * TILE
TOP = 512
MIB = 1 << 20


def hop(value, dy, dx, dc):
    pairs = []
    for y in range(NY):
        for x in range(NX):
            for c in range(NC):
                source = (y * NX + x) * NC + c
                target = ((y + dy) % NY * NX + (x + dx) % NX) * NC + (c + dc) % NC
                pairs.append((source, target))
    return lax.ppermute(value, "tensor", pairs)


def whole_call(kernel, out_shape, *args, scratch=(), flops=0, after=(), hbm=False, limit=24, out_specs=None):
    n_bytes = sum(a.size * a.dtype.itemsize for a in args)
    n, m = len(args), len(after)

    def without_after(*refs):
        kernel(*refs[:n], *refs[n + m :])

    space = pltpu.HBM if hbm else pltpu.VMEM
    return pl.pallas_call(
        without_after,
        out_shape=out_shape,
        in_specs=[pl.BlockSpec(memory_space=space)] * n
        + [pl.BlockSpec(memory_space=pl.ANY)] * m,
        **({"out_specs": out_specs} if out_specs else {}),
        scratch_shapes=scratch,
        compiler_params=pltpu.CompilerParams(vmem_limit_bytes=limit * MIB),
        cost_estimate=pl.CostEstimate(
            flops=(flops or n_bytes) // 5, bytes_accessed=0, transcendentals=0
        ),
    )(*args, *after)


def f32(ref, rows=slice(None), columns=slice(None)):
    return ref[rows, columns].astype(jnp.float32)


def bf(*shape):
    return jax.ShapeDtypeStruct(shape, jnp.bfloat16)


def blocks_kernel(hidden_ref, out_ref, held, in_sems, out_sems):
    n, rows, width = held.shape
    comes, goes = [], []
    for at in range(n):
        columns = slice(at * width, (at + 1) * width)
        comes.append(
            pltpu.make_async_copy(hidden_ref.at[:, columns], held.at[at], in_sems.at[at])
        )
        goes.append(
            pltpu.make_async_copy(
                held.at[at], out_ref.at[at * rows : (at + 1) * rows], out_sems.at[at]
            )
        )
    for copy in comes:
        copy.start()
    for come, go in zip(comes, goes):
        come.wait()
        go.start()
    for copy in goes:
        copy.wait()


def gather_kernel(first, order_ref, rows_ref, out_ref):
    for at in range(0, out_ref.shape[0], 256):
        order = column_of(order_ref, first + at)
        place = lax.broadcasted_iota(jnp.int32, (256, rows_ref.shape[0]), 1)
        pick = jnp.where(place == order, 1.0, 0.0).astype(jnp.bfloat16)
        out_ref[at : at + 256] = jnp.dot(
            pick, rows_ref[...], preferred_element_type=jnp.float32
        ).astype(jnp.bfloat16)


def column_of(order_ref, first):
    one, two = (lax.broadcasted_iota(jnp.int32, (128, 128), axis) for axis in (0, 1))
    halves = []
    for at in (first // 128, first // 128 + 1):
        row = order_ref[at : at + 1].astype(jnp.float32)
        halves.append(jnp.sum(jnp.where(one == two, row, 0.0), axis=1, keepdims=True))
    return jnp.concatenate(halves, axis=0).astype(jnp.int32)


def first_gather_kernel(first, parts, order_ref, rows_ref, held_ref, out_ref, sems):
    step = rows_ref.shape[0] // parts
    copies = []
    for at in range(parts):
        part = slice(at * step, (at + 1) * step)
        copies.append(
            pltpu.make_async_copy(rows_ref.at[part], held_ref.at[part], sems.at[at])
        )
    for copy in copies:
        copy.start()
    order = column_of(order_ref, first)
    total = jnp.zeros(out_ref.shape, jnp.float32)
    for at in range(parts):
        place = lax.broadcasted_iota(jnp.int32, (256, step), 1) + at * step
        pick = jnp.where(place == order, 1.0, 0.0).astype(jnp.bfloat16)
        copies[at].wait()
        total += jnp.dot(
            pick, held_ref[at * step : (at + 1) * step], preferred_element_type=jnp.float32
        )
    out_ref[...] = total.astype(jnp.bfloat16)


def first_gather(order, rows, first, after):
    m, k = rows.shape
    parts = 4
    n = len(after)
    kernel = functools.partial(first_gather_kernel, first, parts)
    return pl.pallas_call(
        lambda order_ref, rows_ref, *refs: kernel(order_ref, rows_ref, *refs[n:]),
        out_shape=[bf(m, k), bf(256, k)],
        in_specs=[pl.BlockSpec(memory_space=pltpu.VMEM)]
        + [pl.BlockSpec(memory_space=pl.ANY)] * (n + 1),
        scratch_shapes=[pltpu.SemaphoreType.DMA((parts,))],
        compiler_params=pltpu.CompilerParams(vmem_limit_bytes=24 * MIB),
        cost_estimate=pl.CostEstimate(
            flops=2 * 256 * m * k // 5, bytes_accessed=0, transcendentals=0
        ),
    )(order, rows, *after)


def gather(order, rows, first, count, after):
    m, k = rows.shape
    return whole_call(
        functools.partial(gather_kernel, first), bf(count, k), order, rows,
        flops=2 * count * m * k, after=after,
    )


def second_gather_kernel(first, order_ref, rows_ref, w_ref, top_ref, out_ref, sem):
    copy = pltpu.make_async_copy(w_ref.at[:TOP], top_ref, sem)
    copy.start()
    gather_kernel(first, order_ref, rows_ref, out_ref)
    copy.wait()


def second_gather(order, rows, first, w, after):
    m, k = rows.shape
    n = len(after)
    kernel = functools.partial(second_gather_kernel, first)
    return pl.pallas_call(
        lambda order_ref, rows_ref, w_ref, *refs: kernel(order_ref, rows_ref, w_ref, *refs[n:]),
        out_shape=[bf(TOP, w.shape[1]), bf(256, k)],
        in_specs=[pl.BlockSpec(memory_space=pltpu.VMEM)] * 2
        + [pl.BlockSpec(memory_space=pl.ANY)] * (n + 1),
        scratch_shapes=[pltpu.SemaphoreType.DMA],
        compiler_params=pltpu.CompilerParams(vmem_limit_bytes=24 * MIB),
        cost_estimate=pl.CostEstimate(
            flops=2 * 256 * m * k // 5, bytes_accessed=0, transcendentals=0
        ),
    )(order, rows, w, *after)


def first_term_kernel(own_ref, sib_ref, own_w, top_w, w_ref, low_w, b1_ref, b2_ref, total, sem):
    copy = pltpu.make_async_copy(w_ref.at[TOP:], low_w, sem)
    copy.start()
    tiles = [
        (slice(at, at + TILE), slice(WA + at, WA + at + TILE)) for at in range(0, WB, TILE)
    ]
    for here, there in tiles:
        one = jnp.dot(own_ref[...], own_w[:, there], preferred_element_type=jnp.float32)
        total[:, here] = one + jnp.dot(
            sib_ref[:, :TOP], top_w[:, there], preferred_element_type=jnp.float32
        )
    copy.wait()
    for here, there in tiles:
        more = total[:, here] + jnp.dot(
            sib_ref[:, TOP:], low_w[:, there], preferred_element_type=jnp.float32
        )
        if here.start < WB1:
            b1_ref[:, here] = more.astype(jnp.bfloat16)
        else:
            b2_ref[:, here.start - WB1 : here.stop - WB1] = more.astype(jnp.bfloat16)


def first_term(own, sib, w_own, w_top, w_sib):
    k, d = w_sib.shape
    return pl.pallas_call(
        first_term_kernel,
        out_shape=[bf(k - TOP, d), bf(256, WB1), bf(256, WB2)],
        in_specs=[pl.BlockSpec(memory_space=pltpu.VMEM)] * 4
        + [pl.BlockSpec(memory_space=pl.ANY)],
        scratch_shapes=[pltpu.VMEM((256, WB), jnp.float32), pltpu.SemaphoreType.DMA],
        compiler_params=pltpu.CompilerParams(vmem_limit_bytes=24 * MIB),
        cost_estimate=pl.CostEstimate(
            flops=4 * 256 * k * WB // 5, bytes_accessed=0, transcendentals=0
        ),
    )(own, sib, w_own, w_top, w_sib)


def term_kernel(ranges, start, own_ref, sib_ref, own_w, top_w, low_w, *outs):
    rows = slice(start, start + 256)
    for first, count, groups in ranges:
        for j in range(count):
            tile = slice((first + j) * TILE, (first + j + 1) * TILE)
            here = slice(j * TILE, (j + 1) * TILE)
            total = jnp.dot(own_ref[rows], own_w[:, tile], preferred_element_type=jnp.float32)
            total += jnp.dot(
                sib_ref[rows, :TOP], top_w[:, tile], preferred_element_type=jnp.float32
            )
            total += jnp.dot(
                sib_ref[rows, TOP:], low_w[:, tile], preferred_element_type=jnp.float32
            )
            total = total.astype(jnp.bfloat16)
            for out, blocks in zip(outs, groups):
                for at, block in enumerate(blocks):
                    out[at * 128 : (at + 1) * 128, here] = total[block * 128 : (block + 1) * 128]
        outs = outs[len(groups) :]


def term(own, sib, start, w, ranges, after):
    k = w[0].shape[0]
    shapes = [bf(128 * len(g), count * TILE) for _, count, groups in ranges for g in groups]
    return whole_call(
        functools.partial(term_kernel, ranges, start), shapes, own, sib, *w,
        flops=4 * 256 * k * TILE * sum(r[1] for r in ranges), after=after,
    )


def left_kernel(row, base_ref, come_ref, out_ref):
    rows = slice(row, row + 128)
    out_ref[:, :WB1] = (f32(base_ref, columns=slice(WB1)) + f32(come_ref, rows)).astype(jnp.bfloat16)
    out_ref[:, WB1:] = base_ref[:, WB1:]


def right_kernel(row, base_ref, come_ref, out_ref):
    rows = slice(row, row + 128)
    out_ref[:, :WB1] = base_ref[:, :WB1]
    out_ref[:, WB1:] = (f32(base_ref, columns=slice(WB1, WB)) + f32(come_ref, rows)).astype(
        jnp.bfloat16
    )


def both_kernel(row, left_ref, y1_ref, right_ref, y3_ref, left_out, right_out):
    left_kernel(row, left_ref, y1_ref, left_out)
    right_kernel(row, right_ref, y3_ref, right_out)


def widen_kernel(left_ref, right_ref, a_ref, x_ref, left_out, right_out):
    left_out[:, :WB] = left_ref[...]
    right_out[:, :WB] = right_ref[...]
    total = f32(a_ref) + f32(x_ref)
    left_out[:, WB:] = total[:, :WA1].astype(jnp.bfloat16)
    right_out[:, WB:] = total[:, WA1:].astype(jnp.bfloat16)


def sums_kernel(a_ref, b_ref, x_ref, a_out, b_out):
    a_out[...] = f32(a_ref) + f32(x_ref, slice(0, 128))
    b_out[...] = f32(b_ref) + f32(x_ref, slice(128, 256))


def to_right_kernel(total_ref, come_ref, out_ref):
    come = f32(come_ref, columns=slice(WB, None))
    out_ref[:, :WA1] = (total_ref[:, :WA1] + come).astype(jnp.bfloat16)
    out_ref[:, WA1:] = total_ref[:, WA1:].astype(jnp.bfloat16)


def to_left_kernel(total_ref, come_ref, out_ref):
    come = f32(come_ref, columns=slice(WB, None))
    out_ref[:, :WA1] = total_ref[:, :WA1].astype(jnp.bfloat16)
    out_ref[:, WA1:] = (total_ref[:, WA1:] + come).astype(jnp.bfloat16)


def across_kernel(a_ref, b_ref, left_ref, right_ref, out_ref):
    c = slice(WB)
    total = f32(b_ref) + f32(left_ref, columns=c) + f32(right_ref, columns=c)
    out_ref[:, :WA] = a_ref[...]
    out_ref[:, WA:] = total.astype(jnp.bfloat16)


def mine_kernel(a_ref, b_ref, left_ref, right_ref, residual_ref, out_ref):
    out_ref[:, :WA] = f32(residual_ref, columns=slice(WA)) + f32(a_ref)
    b = f32(b_ref) + f32(left_ref) + f32(right_ref)
    out_ref[:, WA:] = f32(residual_ref, columns=slice(WA, None)) + b


def last_kernel(mine_ref, across_ref, left_ref, right_ref, head_ref, out_ref, score_ref):
    out_a = f32(across_ref, columns=slice(WA)) + f32(left_ref) + f32(right_ref)
    out_a = (mine_ref[:, :WA] + out_a).astype(jnp.bfloat16)
    out_b = (mine_ref[:, WA:] + f32(across_ref, columns=slice(WA, None))).astype(jnp.bfloat16)
    out_ref[:, :WA] = out_a
    out_ref[:, WA:] = out_b
    wide_a, wide_b = out_a.astype(jnp.float32), out_b.astype(jnp.float32)
    squares = jnp.sum(wide_a * wide_a, axis=1, keepdims=True)
    squares += jnp.sum(wide_b * wide_b, axis=1, keepdims=True)
    scale = lax.rsqrt(squares / out_ref.shape[1] + 1e-5)
    head = head_ref[...].astype(jnp.float32)
    dots = jnp.sum((wide_a * scale) * head[:, :WA], axis=1, keepdims=True)
    dots += jnp.sum((wide_b * scale) * head[:, WA:], axis=1, keepdims=True)
    n = dots.shape[0]
    same = lax.broadcasted_iota(jnp.int32, (n, n), 0) == lax.broadcasted_iota(jnp.int32, (n, n), 1)
    score_ref[...] = jnp.sum(jnp.where(same, dots, 0.0), axis=0, keepdims=True)


def local(hidden, down_weight, residual, row_order, value_head):
    t = lax.axis_index("tensor")
    y, x, core = t // 4, t // 2 % 2, t % 2
    rows, d = residual.shape
    k = down_weight.shape[0]

    blocks = whole_call(
        blocks_kernel, bf(NY * NX * NC * rows, k), hidden,
        scratch=[
            pltpu.VMEM((NY * NX * NC, rows, k), jnp.bfloat16),
            pltpu.SemaphoreType.DMA((NY * NX * NC,)),
            pltpu.SemaphoreType.DMA((NY * NX * NC,)),
        ],
        hbm=True, limit=60,
        out_specs=pl.BlockSpec(memory_space=pltpu.HBM),
    )
    held = lax.all_to_all(blocks, "tensor", split_axis=0, concat_axis=0, tiled=True)
    w_own = down_weight
    w_sib = hop(down_weight, 0, 0, 1)

    order = row_order.reshape(NY, NX, NC, rows)
    order = lax.dynamic_slice_in_dim(jnp.concatenate([order, order], axis=0), y, NY, 0)
    order = jnp.where(x == 0, order[:, ::-1], order)
    order = jnp.where(core == 0, order[:, :, ::-1], order)
    places = [(2, 0), (2, 1), (1, 0), (3, 0), (1, 1), (3, 1), (0, 0), (0, 1)]
    order = jnp.stack([order[p] for p in places], axis=1).reshape(-1, rows)
    own = order.size // 2

    tb1 = A_TILES
    a_stacked = ((0, A_TILES, ((0, 1),)),)
    a_only = ((0, A_TILES, ((0,), (1,))),)
    both = ((0, A_TILES, ((0,), (1,))), (tb1, B1_TILES + B2_TILES, ((0,), (1,))))
    b_only = both[1:]

    held_sib = hop(held, 0, 0, 1)
    held, give2 = first_gather(order, held, 0, (w_sib,))
    sib2 = hop(give2, 0, 0, 1)
    w_top, own2 = second_gather(order, held, own, w_sib, (give2,))
    w_low, b1, b2 = first_term(own2, sib2, w_own, w_top, w_sib)
    w = (w_own, w_top, w_low)
    y1 = hop(b1, 1, 0, 0)
    y3 = hop(b2, 3, 0, 0)
    ax2, ao2 = term(own2, sib2, 0, w, a_only, (b1,))
    x2 = hop(ax2, 0, 1, 0)
    own13x = gather(order, held, own + 256, 256, (ax2,))
    held_sib, sib13x = first_gather(order, held_sib, own + 256, (own13x,))
    ax13 = term(own13x, sib13x, 0, w, a_stacked, ())[0]
    x13 = hop(ax13, 0, 1, 0)
    bx1, bx3 = term(own13x, sib13x, 0, w, b_only, (ax13,))
    t1, t3 = whole_call(
        functools.partial(both_kernel, 0), [bf(128, WB)] * 2, bx1, y1, bx3, y3
    )
    tv1, tv3 = whole_call(
        widen_kernel, [bf(128, WB + WA1), bf(128, WB + WA - WA1)], t1, t3, ao2, x2
    )
    v1 = hop(tv1, 1, 0, 0)
    v3 = hop(tv3, 3, 0, 0)
    own_r = gather(order, held, own + 512, 512, (tv3,))
    sib_r = gather(order, held_sib, own + 512, 512, (own_r,))
    ao1, ao3, bo1, bo3 = term(own_r, sib_r, 0, w, both, ())
    ax0, ao0, bx0, bo0 = term(own_r, sib_r, 256, w, both, (ao1,))
    tu1, tu3 = whole_call(
        functools.partial(both_kernel, 128), [bf(128, WB)] * 2, bo1, y1, bo3, y3, after=(ax0,)
    )
    u1 = hop(tu1, 1, 0, 0)
    u3 = hop(tu3, 3, 0, 0)
    wide = jax.ShapeDtypeStruct((128, WA), jnp.float32)
    s1, s3 = whole_call(sums_kernel, [wide] * 2, ao1, ao3, x13, after=(tu1,))
    across = whole_call(across_kernel, bf(128, d), ax0, bx0, v1, v3, after=(s1,))
    g = hop(across, 0, 1, 0)
    tz1 = whole_call(to_right_kernel, bf(128, WA), s1, v1, after=(across,))
    z1 = hop(tz1, 1, 0, 0)
    tz3 = whole_call(to_left_kernel, bf(128, WA), s3, v3, after=(tz1,))
    z3 = hop(tz3, 3, 0, 0)
    mine = whole_call(
        mine_kernel, jax.ShapeDtypeStruct((128, d), jnp.float32), ao0, bo0, u1, u3, residual,
        after=(tz3,), flops=200 * 10**9,
    )
    layer_out, scores = whole_call(
        last_kernel,
        [bf(rows, d), jax.ShapeDtypeStruct((1, rows), jnp.float32)],
        mine, g, z1, z3, value_head.reshape(1, d),
    )
    return (layer_out, scores.reshape(rows))


def solution(mesh):
    return jax.shard_map(
        local,
        mesh=mesh,
        in_specs=(
            P(("dp", "tensor"), None),
            P("tensor", None),
            P(("dp", "tensor"), None),
            P("dp"),
            P(),
        ),
        out_specs=(P(("dp", "tensor"), None), P(("dp", "tensor"))),
        check_vma=False,
    )
```

```python
import functools

import jax
import jax.numpy as jnp
from jax import lax
from jax.experimental import pallas as pl
from jax.experimental.pallas import tpu as pltpu
from jax.sharding import PartitionSpec as P

NY, NX, NC = 4, 2, 2
TILE = 256
A_TILES, B1_TILES, B2_TILES = 7, 5, 4
WA, WB1, WB2 = A_TILES * TILE, B1_TILES * TILE, B2_TILES * TILE
WB = WB1 + WB2
WA1 = 4 * TILE
TOP = 512
MIB = 1 << 20


def hop(value, dy, dx, dc):
    pairs = []
    for y in range(NY):
        for x in range(NX):
            for c in range(NC):
                source = (y * NX + x) * NC + c
                target = ((y + dy) % NY * NX + (x + dx) % NX) * NC + (c + dc) % NC
                pairs.append((source, target))
    return lax.ppermute(value, "tensor", pairs)


def whole_call(kernel, out_shape, *args, scratch=(), flops=0, after=(), hbm=False, limit=24, out_specs=None):
    n_bytes = sum(a.size * a.dtype.itemsize for a in args)
    n, m = len(args), len(after)

    def without_after(*refs):
        kernel(*refs[:n], *refs[n + m :])

    space = pltpu.HBM if hbm else pltpu.VMEM
    return pl.pallas_call(
        without_after,
        out_shape=out_shape,
        in_specs=[pl.BlockSpec(memory_space=space)] * n
        + [pl.BlockSpec(memory_space=pl.ANY)] * m,
        **({"out_specs": out_specs} if out_specs else {}),
        scratch_shapes=scratch,
        compiler_params=pltpu.CompilerParams(vmem_limit_bytes=limit * MIB),
        cost_estimate=pl.CostEstimate(
            flops=(flops or n_bytes) // 5, bytes_accessed=0, transcendentals=0
        ),
    )(*args, *after)


def f32(ref, rows=slice(None), columns=slice(None)):
    return ref[rows, columns].astype(jnp.float32)


def bf(*shape):
    return jax.ShapeDtypeStruct(shape, jnp.bfloat16)


def blocks_kernel(hidden_ref, out_ref, held, in_sems, out_sems):
    n, rows, width = held.shape
    comes, goes = [], []
    for at in range(n):
        columns = slice(at * width, (at + 1) * width)
        comes.append(
            pltpu.make_async_copy(hidden_ref.at[:, columns], held.at[at], in_sems.at[at])
        )
        goes.append(
            pltpu.make_async_copy(
                held.at[at], out_ref.at[at * rows : (at + 1) * rows], out_sems.at[at]
            )
        )
    for copy in comes:
        copy.start()
    for come, go in zip(comes, goes):
        come.wait()
        go.start()
    for copy in goes:
        copy.wait()


def gather_kernel(first, order_ref, rows_ref, out_ref):
    for at in range(0, out_ref.shape[0], 256):
        order = column_of(order_ref, first + at)
        place = lax.broadcasted_iota(jnp.int32, (256, rows_ref.shape[0]), 1)
        pick = jnp.where(place == order, 1.0, 0.0).astype(jnp.bfloat16)
        out_ref[at : at + 256] = jnp.dot(
            pick, rows_ref[...], preferred_element_type=jnp.float32
        ).astype(jnp.bfloat16)


def column_of(order_ref, first):
    one, two = (lax.broadcasted_iota(jnp.int32, (128, 128), axis) for axis in (0, 1))
    halves = []
    for at in (first // 128, first // 128 + 1):
        row = order_ref[at : at + 1].astype(jnp.float32)
        halves.append(jnp.sum(jnp.where(one == two, row, 0.0), axis=1, keepdims=True))
    return jnp.concatenate(halves, axis=0).astype(jnp.int32)


def first_gather_kernel(first, parts, order_ref, rows_ref, held_ref, out_ref, sems):
    step = rows_ref.shape[0] // parts
    copies = []
    for at in range(parts):
        part = slice(at * step, (at + 1) * step)
        copies.append(
            pltpu.make_async_copy(rows_ref.at[part], held_ref.at[part], sems.at[at])
        )
    for copy in copies:
        copy.start()
    order = column_of(order_ref, first)
    total = jnp.zeros(out_ref.shape, jnp.float32)
    for at in range(parts):
        place = lax.broadcasted_iota(jnp.int32, (256, step), 1) + at * step
        pick = jnp.where(place == order, 1.0, 0.0).astype(jnp.bfloat16)
        copies[at].wait()
        total += jnp.dot(
            pick, held_ref[at * step : (at + 1) * step], preferred_element_type=jnp.float32
        )
    out_ref[...] = total.astype(jnp.bfloat16)


def first_gather(order, rows, first, after):
    m, k = rows.shape
    parts = 4
    n = len(after)
    kernel = functools.partial(first_gather_kernel, first, parts)
    return pl.pallas_call(
        lambda order_ref, rows_ref, *refs: kernel(order_ref, rows_ref, *refs[n:]),
        out_shape=[bf(m, k), bf(256, k)],
        in_specs=[pl.BlockSpec(memory_space=pltpu.VMEM)]
        + [pl.BlockSpec(memory_space=pl.ANY)] * (n + 1),
        scratch_shapes=[pltpu.SemaphoreType.DMA((parts,))],
        compiler_params=pltpu.CompilerParams(vmem_limit_bytes=24 * MIB),
        cost_estimate=pl.CostEstimate(
            flops=2 * 256 * m * k // 5, bytes_accessed=0, transcendentals=0
        ),
    )(order, rows, *after)


def gather(order, rows, first, count, after):
    m, k = rows.shape
    return whole_call(
        functools.partial(gather_kernel, first), bf(count, k), order, rows,
        flops=2 * count * m * k, after=after,
    )


def second_gather_kernel(first, order_ref, rows_ref, w_ref, top_ref, out_ref, sem):
    copy = pltpu.make_async_copy(w_ref.at[:TOP], top_ref, sem)
    copy.start()
    gather_kernel(first, order_ref, rows_ref, out_ref)
    copy.wait()


def second_gather(order, rows, first, w, after):
    m, k = rows.shape
    n = len(after)
    kernel = functools.partial(second_gather_kernel, first)
    return pl.pallas_call(
        lambda order_ref, rows_ref, w_ref, *refs: kernel(order_ref, rows_ref, w_ref, *refs[n:]),
        out_shape=[bf(TOP, w.shape[1]), bf(256, k)],
        in_specs=[pl.BlockSpec(memory_space=pltpu.VMEM)] * 2
        + [pl.BlockSpec(memory_space=pl.ANY)] * (n + 1),
        scratch_shapes=[pltpu.SemaphoreType.DMA],
        compiler_params=pltpu.CompilerParams(vmem_limit_bytes=24 * MIB),
        cost_estimate=pl.CostEstimate(
            flops=2 * 256 * m * k // 5, bytes_accessed=0, transcendentals=0
        ),
    )(order, rows, w, *after)


def first_term_kernel(own_ref, sib_ref, own_w, top_w, w_ref, low_w, b1_ref, b2_ref, total, sem):
    copy = pltpu.make_async_copy(w_ref.at[TOP:], low_w, sem)
    copy.start()
    tiles = [
        (slice(at, at + TILE), slice(WA + at, WA + at + TILE)) for at in range(0, WB, TILE)
    ]
    for here, there in tiles:
        one = jnp.dot(own_ref[...], own_w[:, there], preferred_element_type=jnp.float32)
        total[:, here] = one + jnp.dot(
            sib_ref[:, :TOP], top_w[:, there], preferred_element_type=jnp.float32
        )
    copy.wait()
    for here, there in tiles:
        more = total[:, here] + jnp.dot(
            sib_ref[:, TOP:], low_w[:, there], preferred_element_type=jnp.float32
        )
        if here.start < WB1:
            b1_ref[:, here] = more.astype(jnp.bfloat16)
        else:
            b2_ref[:, here.start - WB1 : here.stop - WB1] = more.astype(jnp.bfloat16)


def first_term(own, sib, w_own, w_top, w_sib):
    k, d = w_sib.shape
    return pl.pallas_call(
        first_term_kernel,
        out_shape=[bf(k - TOP, d), bf(256, WB1), bf(256, WB2)],
        in_specs=[pl.BlockSpec(memory_space=pltpu.VMEM)] * 4
        + [pl.BlockSpec(memory_space=pl.ANY)],
        scratch_shapes=[pltpu.VMEM((256, WB), jnp.float32), pltpu.SemaphoreType.DMA],
        compiler_params=pltpu.CompilerParams(vmem_limit_bytes=24 * MIB),
        cost_estimate=pl.CostEstimate(
            flops=4 * 256 * k * WB // 5, bytes_accessed=0, transcendentals=0
        ),
    )(own, sib, w_own, w_top, w_sib)


def term_kernel(ranges, start, own_ref, sib_ref, own_w, top_w, low_w, *outs):
    rows = slice(start, start + 256)
    for first, count, groups in ranges:
        for j in range(count):
            tile = slice((first + j) * TILE, (first + j + 1) * TILE)
            here = slice(j * TILE, (j + 1) * TILE)
            total = jnp.dot(own_ref[rows], own_w[:, tile], preferred_element_type=jnp.float32)
            total += jnp.dot(
                sib_ref[rows, :TOP], top_w[:, tile], preferred_element_type=jnp.float32
            )
            total += jnp.dot(
                sib_ref[rows, TOP:], low_w[:, tile], preferred_element_type=jnp.float32
            )
            total = total.astype(jnp.bfloat16)
            for out, blocks in zip(outs, groups):
                for at, block in enumerate(blocks):
                    out[at * 128 : (at + 1) * 128, here] = total[block * 128 : (block + 1) * 128]
        outs = outs[len(groups) :]


def term(own, sib, start, w, ranges, after):
    k = w[0].shape[0]
    shapes = [bf(128 * len(g), count * TILE) for _, count, groups in ranges for g in groups]
    return whole_call(
        functools.partial(term_kernel, ranges, start), shapes, own, sib, *w,
        flops=4 * 256 * k * TILE * sum(r[1] for r in ranges), after=after,
    )


def left_kernel(row, base_ref, come_ref, out_ref):
    rows = slice(row, row + 128)
    out_ref[:, :WB1] = (f32(base_ref, columns=slice(WB1)) + f32(come_ref, rows)).astype(jnp.bfloat16)
    out_ref[:, WB1:] = base_ref[:, WB1:]


def right_kernel(row, base_ref, come_ref, out_ref):
    rows = slice(row, row + 128)
    out_ref[:, :WB1] = base_ref[:, :WB1]
    out_ref[:, WB1:] = (f32(base_ref, columns=slice(WB1, WB)) + f32(come_ref, rows)).astype(
        jnp.bfloat16
    )


def both_kernel(row, left_ref, y1_ref, right_ref, y3_ref, left_out, right_out):
    left_kernel(row, left_ref, y1_ref, left_out)
    right_kernel(row, right_ref, y3_ref, right_out)


def widen_kernel(left_ref, right_ref, a_ref, x_ref, left_out, right_out):
    left_out[:, :WB] = left_ref[...]
    right_out[:, :WB] = right_ref[...]
    total = f32(a_ref) + f32(x_ref)
    left_out[:, WB:] = total[:, :WA1].astype(jnp.bfloat16)
    right_out[:, WB:] = total[:, WA1:].astype(jnp.bfloat16)


def sums_kernel(a_ref, b_ref, x_ref, a_out, b_out):
    a_out[...] = f32(a_ref) + f32(x_ref, slice(0, 128))
    b_out[...] = f32(b_ref) + f32(x_ref, slice(128, 256))


def to_right_kernel(total_ref, come_ref, out_ref):
    come = f32(come_ref, columns=slice(WB, None))
    out_ref[:, :WA1] = (total_ref[:, :WA1] + come).astype(jnp.bfloat16)
    out_ref[:, WA1:] = total_ref[:, WA1:].astype(jnp.bfloat16)


def to_left_kernel(total_ref, come_ref, out_ref):
    come = f32(come_ref, columns=slice(WB, None))
    out_ref[:, :WA1] = total_ref[:, :WA1].astype(jnp.bfloat16)
    out_ref[:, WA1:] = (total_ref[:, WA1:] + come).astype(jnp.bfloat16)


def across_kernel(a_ref, b_ref, left_ref, right_ref, out_ref):
    c = slice(WB)
    total = f32(b_ref) + f32(left_ref, columns=c) + f32(right_ref, columns=c)
    out_ref[:, :WA] = a_ref[...]
    out_ref[:, WA:] = total.astype(jnp.bfloat16)


def mine_kernel(a_ref, b_ref, left_ref, right_ref, residual_ref, out_ref):
    out_ref[:, :WA] = f32(residual_ref, columns=slice(WA)) + f32(a_ref)
    b = f32(b_ref) + f32(left_ref) + f32(right_ref)
    out_ref[:, WA:] = f32(residual_ref, columns=slice(WA, None)) + b


def last_kernel(mine_ref, across_ref, left_ref, right_ref, head_ref, out_ref, score_ref):
    out_a = f32(across_ref, columns=slice(WA)) + f32(left_ref) + f32(right_ref)
    out_a = (mine_ref[:, :WA] + out_a).astype(jnp.bfloat16)
    out_b = (mine_ref[:, WA:] + f32(across_ref, columns=slice(WA, None))).astype(jnp.bfloat16)
    out_ref[:, :WA] = out_a
    out_ref[:, WA:] = out_b
    wide_a, wide_b = out_a.astype(jnp.float32), out_b.astype(jnp.float32)
    squares = jnp.sum(wide_a * wide_a, axis=1, keepdims=True)
    squares += jnp.sum(wide_b * wide_b, axis=1, keepdims=True)
    scale = lax.rsqrt(squares / out_ref.shape[1] + 1e-5)
    head = head_ref[...].astype(jnp.float32)
    dots = jnp.sum((wide_a * scale) * head[:, :WA], axis=1, keepdims=True)
    dots += jnp.sum((wide_b * scale) * head[:, WA:], axis=1, keepdims=True)
    n = dots.shape[0]
    same = lax.broadcasted_iota(jnp.int32, (n, n), 0) == lax.broadcasted_iota(jnp.int32, (n, n), 1)
    score_ref[...] = jnp.sum(jnp.where(same, dots, 0.0), axis=0, keepdims=True)


def local(hidden, down_weight, residual, row_order, value_head):
    t = lax.axis_index("tensor")
    y, x, core = t // 4, t // 2 % 2, t % 2
    rows, d = residual.shape
    k = down_weight.shape[0]

    blocks = whole_call(
        blocks_kernel, bf(NY * NX * NC * rows, k), hidden,
        scratch=[
            pltpu.VMEM((NY * NX * NC, rows, k), jnp.bfloat16),
            pltpu.SemaphoreType.DMA((NY * NX * NC,)),
            pltpu.SemaphoreType.DMA((NY * NX * NC,)),
        ],
        hbm=True, limit=60,
        out_specs=pl.BlockSpec(memory_space=pltpu.HBM),
    )
    held = lax.all_to_all(blocks, "tensor", split_axis=0, concat_axis=0, tiled=True)
    w_own = down_weight
    w_sib = hop(down_weight, 0, 0, 1)

    order = row_order.reshape(NY, NX, NC, rows)
    order = lax.dynamic_slice_in_dim(jnp.concatenate([order, order], axis=0), y, NY, 0)
    order = jnp.where(x == 0, order[:, ::-1], order)
    order = jnp.where(core == 0, order[:, :, ::-1], order)
    places = [(2, 0), (2, 1), (1, 0), (3, 0), (1, 1), (3, 1), (0, 0), (0, 1)]
    order = jnp.stack([order[p] for p in places], axis=1).reshape(-1, rows)
    own = order.size // 2

    tb1 = A_TILES
    a_stacked = ((0, A_TILES, ((0, 1),)),)
    a_only = ((0, A_TILES, ((0,), (1,))),)
    both = ((0, A_TILES, ((0,), (1,))), (tb1, B1_TILES + B2_TILES, ((0,), (1,))))
    b_only = both[1:]

    held_sib = hop(held, 0, 0, 1)
    held, give2 = first_gather(order, held, 0, (w_sib,))
    sib2 = hop(give2, 0, 0, 1)
    w_top, own2 = second_gather(order, held, own, w_sib, (give2,))
    w_low, b1, b2 = first_term(own2, sib2, w_own, w_top, w_sib)
    w = (w_own, w_top, w_low)
    y1 = hop(b1, 1, 0, 0)
    y3 = hop(b2, 3, 0, 0)
    ax2, ao2 = term(own2, sib2, 0, w, a_only, (b1,))
    x2 = hop(ax2, 0, 1, 0)
    own13x = gather(order, held, own + 256, 256, (ax2,))
    held_sib, sib13x = first_gather(order, held_sib, own + 256, (own13x,))
    ax13 = term(own13x, sib13x, 0, w, a_stacked, ())[0]
    x13 = hop(ax13, 0, 1, 0)
    bx1, bx3 = term(own13x, sib13x, 0, w, b_only, (ax13,))
    t1, t3 = whole_call(
        functools.partial(both_kernel, 0), [bf(128, WB)] * 2, bx1, y1, bx3, y3
    )
    tv1, tv3 = whole_call(
        widen_kernel, [bf(128, WB + WA1), bf(128, WB + WA - WA1)], t1, t3, ao2, x2
    )
    v1 = hop(tv1, 1, 0, 0)
    v3 = hop(tv3, 3, 0, 0)
    own_r = gather(order, held, own + 512, 512, (tv3,))
    sib_r = gather(order, held_sib, own + 512, 512, (own_r,))
    ao1, ao3, bo1, bo3 = term(own_r, sib_r, 0, w, both, ())
    ax0, ao0, bx0, bo0 = term(own_r, sib_r, 256, w, both, (ao1,))
    tu1, tu3 = whole_call(
        functools.partial(both_kernel, 128), [bf(128, WB)] * 2, bo1, y1, bo3, y3, after=(ax0,)
    )
    u1 = hop(tu1, 1, 0, 0)
    u3 = hop(tu3, 3, 0, 0)
    wide = jax.ShapeDtypeStruct((128, WA), jnp.float32)
    s1, s3 = whole_call(sums_kernel, [wide] * 2, ao1, ao3, x13, after=(tu1,))
    across = whole_call(across_kernel, bf(128, d), ax0, bx0, v1, v3, after=(s1,))
    g = hop(across, 0, 1, 0)
    tz1 = whole_call(to_right_kernel, bf(128, WA), s1, v1, after=(across,))
    z1 = hop(tz1, 1, 0, 0)
    tz3 = whole_call(to_left_kernel, bf(128, WA), s3, v3, after=(tz1,))
    z3 = hop(tz3, 3, 0, 0)
    mine = whole_call(
        mine_kernel, jax.ShapeDtypeStruct((128, d), jnp.float32), ao0, bo0, u1, u3, residual,
        after=(tz3,), flops=200 * 10**9,
    )
    layer_out, scores = whole_call(
        last_kernel,
        [bf(rows, d), jax.ShapeDtypeStruct((1, rows), jnp.float32)],
        mine, g, z1, z3, value_head.reshape(1, d),
    )
    return (layer_out, scores.reshape(rows))


def solution(mesh):
    return jax.shard_map(
        local,
        mesh=mesh,
        in_specs=(
            P(("dp", "tensor"), None),
            P("tensor", None),
            P(("dp", "tensor"), None),
            P("dp"),
            P(),
        ),
        out_specs=(P(("dp", "tensor"), None), P(("dp", "tensor"))),
        check_vma=False,
    )
```
